128 devices in a mesh: section: 16 (over y_lo, x, core), dp: 8 (over y_hi, z).
Axes of the slice: x: 4, y: 4 (y_hi: 2, y_lo: 2; y = y_hi * 2 + y_lo), z: 4, core: 2. Of those that a mesh axis runs over, the one named last changes fastest.
Arguments:
- pending_adjoints: bfloat16 [2, 16, 8, 16, 32, 256], P(None, 'section', 'dp'), may hold values from -6 to 6
- objective_adjoints: bfloat16 [3, 8, 16, 32, 256], P(None, 'dp'), may hold values from -6 to 6
- kept_block_entries: bfloat16 [2, 16, 4, 8, 16, 32, 256], P(None, 'section', None, 'dp'), may hold values from -6 to 6
- kept_early_presums: bfloat16 [2, 16, 4, 8, 16, 32, 256], P(None, 'section', None, 'dp'), may hold values from -6 to 6
- kept_later_presums: bfloat16 [2, 16, 4, 8, 16, 32, 256], P(None, 'section', None, 'dp'), may hold values from -6 to 6
- filter_taps: bfloat16 [2, 16, 2, 9, 256, 256], P(None, 'section'), may hold values from -0.1875 to 0.1875
- slot_timetable: int32 [4, 32], replicated, may hold values from 0 to 3, as said below
Outputs:
- final_grads: bfloat16 [2, 16, 8, 16, 32, 256], P(None, 'section', 'dp')
- weight_grads: float32 [2, 16, 2, 9, 256, 256], P(None, 'section', None, None, 'dp')
The draws below stay inside these ranges and needn't reach their ends.
Inputs may be any that keep to these rules, and one draw needn't show every extreme that they name: `slot_timetable`: in each column the slot rises by one from tick to tick, modulo 4, from a starting slot drawn for each section, so each section visits every slot once.
All inputs are finite; a program needn't handle non-finite values.
Results may differ from the reference program's by a relative error of at most 0.017.
Values may be sent and summed in bfloat16 or wider, within the bound.
No kernel may reach another device: no remote copies, remote signals or barrier semaphores. Data moves between devices by JAX's collectives and lax.ppermute only.
A program may use at most 192 MiB of HBM per device.

```python
import math
import jax
import jax.numpy as jnp
from jax import lax

FEATURE_PLANES = 256
PICTURE_ROWS = 16
PICTURE_COLUMNS = 32
TICKS = 4
SLOTS = 4
LEVELS = 16
NUMBER_OF_BLOCKS = 32
MICRO_PICTURES = 8
N_SECTION = 16


def draw_slot_timetable(key, part):
    starts = jax.random.randint(jax.random.fold_in(key, 17), (NUMBER_OF_BLOCKS,), 0, SLOTS)
    moments = jnp.arange(TICKS, dtype=jnp.int32)[:, None]
    return ((moments + starts[None, :]) % SLOTS).astype(jnp.int32)


def shard_levels(own_key, extent, split, low, high):
    def one(axis_at, shards_of):
        steps = jax.random.uniform(jax.random.fold_in(jax.random.fold_in(own_key, 6), axis_at), (shards_of,), jnp.float32, low / len(split), high / len(split))
        return jnp.repeat(jnp.exp(steps), extent[axis_at] // shards_of).reshape((-1,) + (1,) * (len(extent) - axis_at - 1))

    factor_of = one(*split[0])
    for cut in split[1:]:
        factor_of = factor_of * one(*cut)
    return factor_of


def normal_values(own_key, shape, width, most, shards=(), kind=jnp.bfloat16):
    result = jax.random.normal(own_key, shape, jnp.float32) * width
    if len(shards) > 0:
        result = shard_levels(own_key, shape, shards, -0.22, 0.18) * result
    return jnp.clip(result, min=-most, max=most).astype(kind)


def setup_inputs(seed: int = 0) -> dict:
    streams_of = jax.random.split(jax.random.key(seed), 8)
    pending_adjoints = normal_values(streams_of[0], (2, LEVELS, MICRO_PICTURES, PICTURE_ROWS, PICTURE_COLUMNS, FEATURE_PLANES), 1.0, 6.0, ((1, 16), (2, 8)))
    objective_adjoints = normal_values(streams_of[1], (TICKS - 1, MICRO_PICTURES, PICTURE_ROWS, PICTURE_COLUMNS, FEATURE_PLANES), 1.0, 6.0, ((1, 8),))
    kept_block_entries = normal_values(streams_of[2], (2, LEVELS, SLOTS, MICRO_PICTURES, PICTURE_ROWS, PICTURE_COLUMNS, FEATURE_PLANES), 1.0, 6.0, ((1, 16), (3, 8)))
    kept_early_presums = normal_values(streams_of[3], (2, LEVELS, SLOTS, MICRO_PICTURES, PICTURE_ROWS, PICTURE_COLUMNS, FEATURE_PLANES), 1.0, 6.0, ((1, 16), (3, 8)))
    kept_later_presums = normal_values(streams_of[4], (2, LEVELS, SLOTS, MICRO_PICTURES, PICTURE_ROWS, PICTURE_COLUMNS, FEATURE_PLANES), 1.0, 6.0, ((1, 16), (3, 8)))
    filter_taps = normal_values(streams_of[5], (2, LEVELS, 2, 9, FEATURE_PLANES, FEATURE_PLANES), (9 * FEATURE_PLANES // 2) ** -0.5, 0.1875, ((1, 16),))
    slot_timetable = draw_slot_timetable(jax.random.fold_in(streams_of[7], 71), 0)
    return dict(pending_adjoints=pending_adjoints, objective_adjoints=objective_adjoints, kept_block_entries=kept_block_entries, kept_early_presums=kept_early_presums, kept_later_presums=kept_later_presums, filter_taps=filter_taps, slot_timetable=slot_timetable)


def patches(field):
    padded = jnp.pad(field, ((0, 0), (1, 1), (1, 1), (0, 0)))
    rows_n = field.shape[1]
    cols_n = field.shape[2]
    views = [padded[:, row_off:row_off + rows_n, col_off:col_off + cols_n, :] for row_off in range(3) for col_off in range(3)]
    return jnp.stack(views, axis=3).reshape(-1, 9 * field.shape[3])

def flipped(kernel):
    return jnp.swapaxes(kernel[::-1], 1, 2).reshape(-1, kernel.shape[2])

def contract_pixels(left, right):
    return lax.dot_general(left, right, (((0,), (0,)), ((), ())), preferred_element_type=jnp.float32)

def section_backward(kernels, inp, pre_one, pre_two, incoming, skipped):
    shape = inp.shape
    chans = shape[3]
    upper_mask = (pre_two > 0).astype(jnp.float32)
    grad_two = ((incoming.astype(jnp.float32) + skipped.astype(jnp.float32)) * upper_mask).astype(jnp.bfloat16)
    activated = jnp.maximum(pre_one, jnp.zeros_like(pre_one))
    wg_two = contract_pixels(patches(activated), grad_two.reshape(-1, chans))
    back_two = jnp.dot(patches(grad_two), flipped(kernels[1]), preferred_element_type=jnp.float32)
    lower_mask = (pre_one > 0).astype(jnp.float32).reshape(-1, chans)
    grad_one = (back_two * lower_mask).astype(jnp.bfloat16)
    wg_one = contract_pixels(patches(inp), grad_one)
    out_grad = jnp.dot(patches(grad_one.reshape(shape)), flipped(kernels[0]), preferred_element_type=jnp.float32)
    out_grad = out_grad.astype(jnp.bfloat16).reshape(shape)
    return (out_grad, jnp.stack([wg_one, wg_two]).reshape(2, 9, chans, chans))

def flat_sections(array):
    return array.reshape((array.shape[0] * array.shape[1],) + array.shape[2:])

def reference(pending_adjoints, objective_adjoints, kept_block_entries, kept_early_presums, kept_later_presums, filter_taps, slot_timetable):
    levels = N_SECTION
    adjoint_propagate = flat_sections(pending_adjoints)
    bypass_connections = jnp.zeros_like(adjoint_propagate)
    taps_flat = flat_sections(filter_taps)
    entries_flat = flat_sections(kept_block_entries)
    early_flat = flat_sections(kept_early_presums)
    later_flat = flat_sections(kept_later_presums)
    total = jnp.zeros(taps_flat.shape, jnp.float32)
    for moment in range(TICKS):

        def per_section(items):
            kernels, inputs_all, pre_all, post_all, incoming, skipped, slot_index = items
            inp = lax.dynamic_index_in_dim(inputs_all, slot_index, 0, keepdims=False)
            pre_one = lax.dynamic_index_in_dim(pre_all, slot_index, 0, keepdims=False)
            pre_two = lax.dynamic_index_in_dim(post_all, slot_index, 0, keepdims=False)
            return section_backward(kernels, inp, pre_one, pre_two, incoming, skipped)
        out_grad, wgrad = lax.map(per_section, (taps_flat, entries_flat, early_flat, later_flat, adjoint_propagate, bypass_connections, slot_timetable[moment].astype(jnp.int32)))
        total = total + wgrad
        if moment < TICKS - 1:
            enc_out = out_grad[:levels]
            dec_out = out_grad[levels:]
            enc_next = jnp.concatenate([enc_out[1:], dec_out[levels - 1:levels]], axis=0)
            dec_next = jnp.concatenate([objective_adjoints[moment][None], dec_out[:levels - 1]], axis=0)
            adjoint_propagate = jnp.concatenate([enc_next, dec_next], axis=0)
            enc_skip = jnp.concatenate([dec_out[:levels - 1], jnp.zeros_like(dec_out[:1])], axis=0)
            bypass_connections = jnp.concatenate([enc_skip, jnp.zeros_like(dec_out)], axis=0)
    scale = 1.0 / math.sqrt(TICKS * MICRO_PICTURES * PICTURE_ROWS * PICTURE_COLUMNS)
    final_grads = out_grad.reshape(pending_adjoints.shape)
    weight_grads = (total * scale).reshape(filter_taps.shape)
    return (final_grads, weight_grads)
```

```python
import functools
import math

import jax
import jax.numpy as jnp
from jax import lax
from jax.experimental import pallas as pl
from jax.experimental.pallas import tpu as pltpu
from jax.sharding import PartitionSpec as P

TICKS = 4
ROWS = 16
COLS = 32
PIX = ROWS * COLS
CH = 256
DP = 8
SHARE = CH // DP
BF = jnp.bfloat16
F32 = jnp.float32
NT = (((1,), (1,)), ((), ()))

PAIRS = {
    "a": [(d, (d & 4) + ((d & 3) ^ 1)) for d in range(DP)],
    "b": [(d, (d & 4) + 3 - (d & 3)) for d in range(DP)],
    "y": [(d, d ^ 4) for d in range(DP)],
}
ORDERS = ("aby", "bya", "yab")

VM = pl.BlockSpec(memory_space=pltpu.VMEM)
SM = pl.BlockSpec(memory_space=pltpu.SMEM)
LEVEL_AT = 8
REPLICA_AT = 9


def params(mib):
    return pltpu.CompilerParams(vmem_limit_bytes=mib << 20)


def cost(matmuls, nbytes):
    return pl.CostEstimate(flops=matmuls * 2 * PIX * 9 * CH * CH, bytes_accessed=nbytes, transcendentals=0)


def clear_edges(win):
    edge = jnp.zeros((3, COLS, CH), BF)
    win[:, 0:COLS, :] = edge
    win[:, COLS + PIX : 2 * COLS + PIX, :] = edge


def fill_windows(win, field):
    col = lax.broadcasted_iota(jnp.int32, field.shape, 0) & (COLS - 1)
    win[0, COLS : COLS + PIX, :] = jnp.where(col == 0, 0.0, pltpu.roll(field, 1, 0)).astype(BF)
    win[1, COLS : COLS + PIX, :] = field.astype(BF)
    win[2, COLS : COLS + PIX, :] = jnp.where(col == COLS - 1, 0.0, pltpu.roll(field, PIX - 1, 0)).astype(BF)


def tap_of(win, k):
    dy, dx = divmod(k, 3)
    return win[dx, dy * COLS : dy * COLS + PIX, :]


def conv(win, taps, base):
    total = None
    for k in range(9):
        term = lax.dot_general(tap_of(win, k), taps[base + 8 - k], NT, preferred_element_type=F32)
        total = term if total is None else total + term
    return total


def add_two(meta, pre2, half, tick, first, second, objective):
    a = first[...].astype(F32)
    if second is not None:
        a = a + second[...].astype(F32)
    if objective is not None:
        a = jnp.where(meta[LEVEL_AT] == 0, objective[tick - 1].astype(F32), a)
    slot = half * 4 + meta[4 * half + tick]
    return jnp.where(pre2[slot] > 0, a, 0.0)


def chain_kernel(half, tick, n_in, *refs):
    meta, pre1, pre2, taps = refs[:4]
    given = refs[4 : 4 + n_in]
    out, g2_out, g1_out, win = refs[4 + n_in :]
    clear_edges(win)
    if tick == 0:
        g2 = add_two(meta, pre2, half, tick, given[0], None, None)
    elif half == 0:
        g2 = add_two(meta, pre2, half, tick, given[0], given[1], None)
    else:
        g2 = add_two(meta, pre2, half, tick, given[0], None, given[1])
    g2_out[...] = g2.astype(BF)
    fill_windows(win, g2)
    slot = half * 4 + meta[4 * half + tick]
    g1 = jnp.where(pre1[slot] > 0, conv(win, taps, 18 * half + 9), 0.0)
    g1_out[...] = g1.astype(BF)
    fill_windows(win, g1)
    out[...] = conv(win, taps, 18 * half).astype(BF)


def chain(half, tick, meta, pre1, pre2, taps, *given):
    field = jax.ShapeDtypeStruct((PIX, CH), BF)
    return pl.pallas_call(
        functools.partial(chain_kernel, half, tick, len(given)),
        out_shape=(field,) * 3,
        in_specs=[SM] + [VM] * (3 + len(given)),
        out_specs=(VM,) * 3,
        scratch_shapes=[pltpu.VMEM((3, PIX + 2 * COLS, CH), BF)],
        compiler_params=params(8),
        cost_estimate=cost(2, 1 << 20),
        name=f"chain_{half}_{tick}",
    )(meta, pre1, pre2, taps, *given)


def tap_grads(win, x, field):
    fill_windows(win, field)
    xt = x.T
    for k in range(9):
        yield k, jnp.dot(xt, tap_of(win, 8 - k), preferred_element_type=F32)


def wgrad_kernel(half, tick, meta, entries, pre1, g2, g1, *refs):
    if tick == 0:
        new1, new2, win = refs
        old1 = old2 = None
    else:
        old1, old2, new1, new2, win = refs
    clear_edges(win)
    slot = half * 4 + meta[4 * half + tick]
    act = jnp.maximum(pre1[slot], jnp.zeros((), BF))
    for k, term in tap_grads(win, act, g2[...].astype(F32)):
        new2[k] = term if old2 is None else old2[k] + term
    for k, term in tap_grads(win, entries[slot], g1[...].astype(F32)):
        new1[k] = term if old1 is None else old1[k] + term


def wgrad(half, tick, meta, entries, pre1, g2, g1, sums):
    shape = jax.ShapeDtypeStruct((9, CH, CH), F32)
    return pl.pallas_call(
        functools.partial(wgrad_kernel, half, tick),
        out_shape=(shape,) * 2,
        in_specs=[SM] + [VM] * (4 + len(sums)),
        out_specs=(VM,) * 2,
        scratch_shapes=[pltpu.VMEM((3, PIX + 2 * COLS, CH), BF)],
        input_output_aliases={5: 0, 6: 1} if sums else {},
        compiler_params=params(8),
        cost_estimate=cost(2, 1 << 20),
        name=f"wgrad_{half}_{tick}",
    )(meta, entries, pre1, g2, g1, *sums)


def replica_at(me, order, r):
    bit = {order[i]: (r >> (2 - i)) & 1 for i in range(3)}
    y = (me >> 2) & 1
    z = me & 3
    beta = (z >> 1) & 1
    alpha = (z & 1) ^ beta
    alpha = alpha ^ bit["a"]
    beta = beta ^ bit["b"]
    return (y ^ bit["y"]) * 4 + 2 * beta + (alpha ^ beta)


def put_shares(me, staged, k, sends, keeps, half):
    o, at = divmod(k, 3)
    for r in range(DP):
        row = pl.multiple_of(replica_at(me, ORDERS[o], r) * SHARE, SHARE)
        share = staged[k, pl.ds(row, SHARE), :].astype(BF)
        if r >= 4:
            sends[o][r - 4, half, at] = share
        else:
            keeps[o][r, half, at] = share


def last_two_kernel(meta, pre1, pre2, objective, above, dec_out, below, sums_enc, sums_dec, *refs):
    sends, keeps = refs[0:3], refs[3:6]
    g2_enc, g2_dec = refs[6:8]
    win, staged = refs[8:]
    clear_edges(win)
    tick = TICKS - 1
    me = meta[REPLICA_AT]
    for half in (1, 0):
        if half:
            g2 = add_two(meta, pre2, half, tick, below, None, objective)
        else:
            g2 = add_two(meta, pre2, half, tick, above, dec_out, None)
        (g2_enc, g2_dec)[half][...] = g2.astype(BF)
        slot = half * 4 + meta[4 * half + tick]
        act = jnp.maximum(pre1[slot], jnp.zeros((), BF))
        old = (sums_enc, sums_dec)[half]
        for k, term in tap_grads(win, act, g2):
            staged[k] = old[k] + term
            put_shares(me, staged, k, sends, keeps, half)


def last_one_kernel(meta, pre1, entries, taps, g2_enc, g2_dec, sums_enc, sums_dec, *refs):
    sends, keeps = refs[0:3], refs[3:6]
    g1_enc, g1_dec = refs[6:8]
    win, staged = refs[8:]
    clear_edges(win)
    tick = TICKS - 1
    me = meta[REPLICA_AT]
    for half in (1, 0):
        fill_windows(win, (g2_enc, g2_dec)[half][...].astype(F32))
        slot = half * 4 + meta[4 * half + tick]
        g1 = jnp.where(pre1[slot] > 0, conv(win, taps, 18 * half + 9), 0.0)
        (g1_enc, g1_dec)[half][...] = g1.astype(BF)
        old = (sums_enc, sums_dec)[half]
        for k, term in tap_grads(win, entries[slot], g1):
            staged[k] = old[k] + term
            put_shares(me, staged, k, sends, keeps, half)


def last_out_kernel(taps, g1_enc, g1_dec, out, win):
    clear_edges(win)
    for half in (1, 0):
        fill_windows(win, (g1_enc, g1_dec)[half][...].astype(F32))
        out[half] = conv(win, taps, 18 * half).astype(BF)


def last(kernel, name, matmuls, *given):
    part = jax.ShapeDtypeStruct((4, 2, 3, SHARE, CH), BF)
    field = jax.ShapeDtypeStruct((PIX, CH), BF)
    outs = pl.pallas_call(
        kernel,
        out_shape=(part,) * 6 + (field,) * 2,
        in_specs=[SM] + [VM] * (len(given) - 1),
        out_specs=(VM,) * 8,
        scratch_shapes=[pltpu.VMEM((3, PIX + 2 * COLS, CH), BF), pltpu.VMEM((9, CH, CH), F32)],
        compiler_params=params(12),
        cost_estimate=cost(matmuls, 1 << 20),
        name=name,
    )(*given)
    return outs[0:3], outs[3:6], outs[6:8]


def last_out(taps, g1s):
    return pl.pallas_call(
        last_out_kernel,
        out_shape=jax.ShapeDtypeStruct((2, PIX, CH), BF),
        in_specs=[VM] * 3,
        out_specs=VM,
        scratch_shapes=[pltpu.VMEM((3, PIX + 2 * COLS, CH), BF)],
        compiler_params=params(8),
        cost_estimate=cost(2, 1 << 20),
        name="last_out",
    )(taps, *g1s)


def fold_kernel(keep, got, send, left):
    half = keep.shape[0] // 2
    total = keep[...].astype(F32) + got[...].astype(F32)
    left[...] = total[:half].astype(BF)
    send[...] = total[half:].astype(BF)


def fold(keep, got):
    shape = (keep.shape[0] // 2,) + keep.shape[1:]
    part = jax.ShapeDtypeStruct(shape, BF)
    return pl.pallas_call(
        fold_kernel,
        out_shape=(part,) * 2,
        in_specs=[VM] * 2,
        out_specs=(VM,) * 2,
        compiler_params=params(4),
        name="fold",
    )(keep, got)


def finish_kernel(scale, *refs):
    out = refs[-1]
    for piece in range(2):
        for o in range(3):
            keep, got = refs[4 * o + 2 * piece : 4 * o + 2 * piece + 2]
            total = keep[0].astype(F32) + got[0].astype(F32)
            for half in range(2):
                out[half, 1 - piece, 3 * o : 3 * o + 3] = total[half] * scale


def finish(scale, parts):
    return pl.pallas_call(
        functools.partial(finish_kernel, scale),
        out_shape=jax.ShapeDtypeStruct((2, 2, 9, SHARE, CH), F32),
        in_specs=[VM] * len(parts),
        out_specs=VM,
        compiler_params=params(4),
        name="finish",
    )(*parts)


def shifted(block, distance):
    devices = range(lax.axis_size("section"))
    route = [(i - distance, i) for i in devices if i - distance in devices]
    return lax.ppermute(block, "section", route)


def exchange(block, step):
    return lax.ppermute(block, "dp", PAIRS[step])


def on_device(
    pending_adjoints,
    objective_adjoints,
    kept_block_entries,
    kept_early_presums,
    kept_later_presums,
    filter_taps,
    slot_timetable,
):
    levels = lax.axis_size("section")
    level = lax.axis_index("section")
    replica = lax.axis_index("dp")
    enc_slots = lax.dynamic_index_in_dim(slot_timetable, level, 1, keepdims=False)
    dec_slots = lax.dynamic_index_in_dim(slot_timetable, level + levels, 1, keepdims=False)
    meta = jnp.concatenate([enc_slots, dec_slots, jnp.stack([level, replica]).astype(jnp.int32)])
    entries = kept_block_entries.reshape(8, PIX, CH)
    pre1 = kept_early_presums.reshape(8, PIX, CH)
    pre2 = kept_later_presums.reshape(8, PIX, CH)
    taps = filter_taps.reshape(36, CH, CH)
    pending = pending_adjoints.reshape(2, PIX, CH)
    objective = objective_adjoints.reshape(TICKS - 1, PIX, CH)

    enc_sums = dec_sums = ()
    enc_given = (pending[0],)
    dec_given = (pending[1],)
    for tick in range(TICKS - 1):
        dec_out, dec_g2, dec_g1 = chain(1, tick, meta, pre1, pre2, taps, *dec_given)
        below = shifted(dec_out, 1)
        enc_out, enc_g2, enc_g1 = chain(0, tick, meta, pre1, pre2, taps, *enc_given)
        above = shifted(enc_out, -1)
        dec_sums = wgrad(1, tick, meta, entries, pre1, dec_g2, dec_g1, dec_sums)
        enc_sums = wgrad(0, tick, meta, entries, pre1, enc_g2, enc_g1, enc_sums)
        dec_given = (below, objective)
        enc_given = (above, dec_out)

    sends2, keeps2, g2s = last(
        last_two_kernel, "last_two", 2, meta, pre1, pre2, objective, above, dec_out, below, enc_sums[1], dec_sums[1]
    )
    gots2 = [exchange(sends2[o], ORDERS[o][0]) for o in range(3)]
    sends1, keeps1, g1s = last(
        last_one_kernel, "last_one", 4, meta, pre1, entries, taps, *g2s, enc_sums[0], dec_sums[0]
    )
    gots1 = [exchange(sends1[o], ORDERS[o][0]) for o in range(3)]
    final = last_out(taps, g1s)

    parts = []
    for o in range(3):
        for keep, got in ((keeps2[o], gots2[o]), (keeps1[o], gots1[o])):
            for step in ORDERS[o][1:]:
                send, keep = fold(keep, got)
                got = exchange(send, step)
            parts += [keep, got]
    scale = 1.0 / math.sqrt(TICKS * DP * PIX)
    grads = finish(scale, parts)
    return (
        final.reshape(2, 1, 1, ROWS, COLS, CH),
        grads.reshape(2, 1, 2, 9, SHARE, CH),
    )


def solution(mesh):
    placed = (
        P(None, "section", "dp", None, None, None),
        P(None, "dp", None, None, None),
        P(None, "section", None, "dp", None, None, None),
        P(None, "section", None, "dp", None, None, None),
        P(None, "section", None, "dp", None, None, None),
        P(None, "section", None, None, None, None),
        P(),
    )
    return jax.shard_map(
        on_device,
        mesh=mesh,
        in_specs=placed,
        out_specs=(
            P(None, "section", "dp", None, None, None),
            P(None, "section", None, None, "dp", None),
        ),
        check_vma=False,
    )
```

```python
import functools
import math

import jax
import jax.numpy as jnp
from jax import lax
from jax.experimental import pallas as pl
from jax.experimental.pallas import tpu as pltpu
from jax.sharding import PartitionSpec as P

TICKS = 4
ROWS = 16
COLS = 32
PIX = ROWS * COLS
CH = 256
DP = 8
COST = 2 * 512 * 9 * 256 * 256
FOLD_COST = 16
SHARE = CH // DP
BF = jnp.bfloat16
F32 = jnp.float32
NT = (((1,), (1,)), ((), ()))

PAIRS = {
    "a": [(d, (d & 4) + ((d & 3) ^ 1)) for d in range(DP)],
    "b": [(d, (d & 4) + 3 - (d & 3)) for d in range(DP)],
    "y": [(d, d ^ 4) for d in range(DP)],
}
ORDERS = ("aby", "bya", "yab")

VM = pl.BlockSpec(memory_space=pltpu.VMEM)
SM = pl.BlockSpec(memory_space=pltpu.SMEM)
HB = pl.BlockSpec(memory_space=pltpu.HBM)
FIELD = jax.ShapeDtypeStruct((PIX, CH), BF)
SUMS = jax.ShapeDtypeStruct((9, CH, CH), F32)
WINDOWS = pltpu.VMEM((3, PIX + 2 * COLS, CH), BF)


def half_of(role):
    odd = lax.axis_index("section") & 1
    return odd if role == 0 else 1 - odd


def call(kernel, name, given, outs, specs=None, scratch=(), mib=8, aliases={}, ops=1):
    return pl.pallas_call(
        kernel,
        out_shape=outs,
        in_specs=specs or [VM] * len(given),
        out_specs=jax.tree.map(lambda _: VM, outs),
        scratch_shapes=list(scratch),
        input_output_aliases=aliases,
        compiler_params=pltpu.CompilerParams(vmem_limit_bytes=mib << 20),
        cost_estimate=pl.CostEstimate(flops=ops * COST, bytes_accessed=1024, transcendentals=0),
        name=name,
    )(*given)


def clear_edges(win):
    edge = jnp.zeros((3, COLS, CH), BF)
    win[:, 0:COLS, :] = edge
    win[:, COLS + PIX : 2 * COLS + PIX, :] = edge


def fill_windows(win, field):
    clear_edges(win)
    col = lax.broadcasted_iota(jnp.int32, field.shape, 0) & (COLS - 1)
    win[0, COLS : COLS + PIX, :] = jnp.where(col == 0, 0.0, pltpu.roll(field, 1, 0)).astype(BF)
    win[1, COLS : COLS + PIX, :] = field.astype(BF)
    win[2, COLS : COLS + PIX, :] = jnp.where(col == COLS - 1, 0.0, pltpu.roll(field, PIX - 1, 0)).astype(BF)


def tap_of(win, k):
    dy, dx = divmod(k, 3)
    return win[dx, dy * COLS : dy * COLS + PIX, :]


def conv(win, taps, base):
    total = None
    for k in range(9):
        term = lax.dot_general(tap_of(win, k), taps[base + 8 - k], NT, preferred_element_type=F32)
        total = term if total is None else total + term
    return total


def slot_of(table, role, tick):
    half = half_of(role)
    column = half * lax.axis_size("section") + lax.axis_index("section")
    place = lax.broadcasted_iota(jnp.int32, table.shape, 1) == column
    row = lax.broadcasted_iota(jnp.int32, table.shape, 0) == tick
    return half * 4 + jnp.sum(jnp.where(place & row, table[...], 0))


def add_up(role, tick, got, other, objective):
    total = got[...].astype(F32)
    encoder = half_of(role) == 0
    total = total + jnp.where(encoder, other[...].astype(F32), 0.0)
    if role == 1:
        first = lax.axis_index("section") == 0
        total = jnp.where(first, objective[tick - 1].astype(F32), total)
    return total


def early_of_kernel(role, mask, taps, g2, g1_out, win):
    fill_windows(win, g2[...].astype(F32))
    g1_out[...] = jnp.where(mask[...] > 0, conv(win, taps, 18 * half_of(role) + 9), 0.0).astype(BF)


def early_kernel(role, tick, table, pre1, pre2, taps, *refs):
    given = refs[:-3]
    g2_out, g1_out, win = refs[-3:]
    slot = slot_of(table, role, tick)
    g2 = add_up(role, tick, *given, *([None] * (3 - len(given))))
    g2 = jnp.where(pre2[slot] > 0, g2, 0.0)
    g2_out[...] = g2.astype(BF)
    fill_windows(win, g2)
    g1_out[...] = jnp.where(pre1[slot] > 0, conv(win, taps, 18 * half_of(role) + 9), 0.0).astype(BF)


def late_kernel(role, taps, g1, out, win):
    fill_windows(win, g1[...].astype(F32))
    out[...] = conv(win, taps, 18 * half_of(role)).astype(BF)


def tap_grads(win, x, field):
    fill_windows(win, field)
    xt = x.T
    for k in range(9):
        yield k, jnp.dot(xt, tap_of(win, 8 - k), preferred_element_type=F32)


def left_side(which, saved, slot):
    x = saved[slot]
    return jnp.maximum(x, jnp.zeros((), BF)) if which else x


def wgrad_kernel(which, role, tick, table, saved, field, *refs):
    old = None if tick == 0 else refs[0]
    new, win = refs[-2:]
    x = left_side(which, saved, slot_of(table, role, tick))
    for k, term in tap_grads(win, x, field[...].astype(F32)):
        new[k] = term if old is None else old[k] + term


def replica_at(order, r):
    me = lax.axis_index("dp")
    bit = {order[i]: (r >> (2 - i)) & 1 for i in range(3)}
    y = (me >> 2) & 1
    z = me & 3
    beta = (z >> 1) & 1
    alpha = (z & 1) ^ beta
    alpha = alpha ^ bit["a"]
    beta = beta ^ bit["b"]
    return (y ^ bit["y"]) * 4 + 2 * beta + (alpha ^ beta)


def put_shares(staged, k, sends, keeps, role):
    o, at = divmod(k, 3)
    for r in range(DP):
        row = pl.multiple_of(replica_at(ORDERS[o], r) * SHARE, SHARE)
        share = staged[k, pl.ds(row, SHARE), :].astype(BF)
        if r >= 4:
            sends[o][r - 4, role, at] = share
        else:
            keeps[o][r, role, at] = share


def last_two_kernel(table, pre1, pre2, objective, *refs):
    given, olds = refs[:4], refs[4:6]
    sends, keeps, g2s = refs[6:9], refs[9:12], refs[12:14]
    wins, staged = refs[14:16], refs[16:18]
    tick = TICKS - 1
    for role in range(2):
        slot = slot_of(table, role, tick)
        g2 = add_up(role, tick, given[role], given[3 - role], objective)
        g2 = jnp.where(pre2[slot] > 0, g2, 0.0)
        g2s[role][...] = g2.astype(BF)
        x = left_side(1, pre1, slot)
        for k, term in tap_grads(wins[role], x, g2):
            staged[role][k] = olds[role][k] + term
            put_shares(staged[role], k, sends, keeps, role)


def last_early_kernel(role, table, pre1, taps, g2, g1_out, win):
    slot = slot_of(table, role, TICKS - 1)
    fill_windows(win, g2[...].astype(F32))
    g1_out[...] = jnp.where(pre1[slot] > 0, conv(win, taps, 18 * half_of(role) + 9), 0.0).astype(BF)


def last_one_kernel(table, entries, *refs):
    g1s, olds = refs[:2], refs[2:4]
    sends, keeps = refs[4:7], refs[7:10]
    wins, staged = refs[10:12], refs[12:14]
    for role in range(2):
        x = left_side(0, entries, slot_of(table, role, TICKS - 1))
        for k, term in tap_grads(wins[role], x, g1s[role][...].astype(F32)):
            staged[role][k] = olds[role][k] + term
            put_shares(staged[role], k, sends, keeps, role)


def last_late_kernel(taps, g1_zero, g1_one, out, *wins):
    for role in range(2):
        half = half_of(role)
        fill_windows(wins[role], (g1_zero, g1_one)[role][...].astype(F32))
        out[half] = conv(wins[role], taps, 18 * half).astype(BF)


def fold_in(keep, got, send, left):
    half = keep.shape[0] // 2
    total = keep[...].astype(F32) + got[...].astype(F32)
    left[...] = total[:half].astype(BF)
    send[...] = total[half:].astype(BF)


def fold_two_kernel(*refs):
    for o in range(3):
        keep, got, send, left = refs[o::3]
        fold_in(keep, got, send.at[:, 1], left.at[:, 1])


def fold_one_kernel(keep, got, old_send, old_left, send, left):
    del old_send, old_left
    fold_in(keep, got, send.at[:, 0], left.at[:, 0])


def finish_kernel(scale, *refs):
    out = refs[-1]
    for o in range(3):
        keep, got = refs[2 * o : 2 * o + 2]
        total = keep[0].astype(F32) + got[0].astype(F32)
        for role in range(2):
            half = half_of(role)
            for piece in range(2):
                out[half, piece, 3 * o : 3 * o + 3] = total[piece, role] * scale


def relay(block, role):
    levels = lax.axis_size("section")
    pairs = [(i, i + 1) for i in range(1 - role, levels - 1, 2)]
    return lax.ppermute(block, "section", pairs + [(b, a) for a, b in pairs])


def exchange(block, step):
    return lax.ppermute(block, "dp", PAIRS[step])


def on_device(
    pending_adjoints,
    objective_adjoints,
    kept_block_entries,
    kept_early_presums,
    kept_later_presums,
    filter_taps,
    slot_timetable,
):
    table = slot_timetable
    entries = kept_block_entries.reshape(8, PIX, CH)
    pre1 = kept_early_presums.reshape(8, PIX, CH)
    pre2 = kept_later_presums.reshape(8, PIX, CH)
    taps = filter_taps.reshape(36, CH, CH)
    pending = pending_adjoints.reshape(2, PIX, CH)
    objective = objective_adjoints.reshape(TICKS - 1, PIX, CH)
    windows = [WINDOWS]

    sums1, sums2 = [(), ()], [(), ()]
    gots = outs = None
    for tick in range(TICKS - 1):
        g2s, g1s, new_outs, new_gots = [], [], [], []
        for role in range(2):
            if tick == 0:
                half = half_of(role)
                slot = 4 * half + table[0, half * lax.axis_size("section") + lax.axis_index("section")]
                field = lax.dynamic_index_in_dim(pending, half, 0, keepdims=False)
                g2 = jnp.where(lax.dynamic_index_in_dim(pre2, slot, 0, keepdims=False) > 0, field, jnp.zeros((), BF))
                mask = lax.dynamic_index_in_dim(pre1, slot, 0, keepdims=False)
                g1 = call(
                    functools.partial(early_of_kernel, role),
                    f"early_{role}_0",
                    (mask, taps, g2),
                    FIELD,
                    scratch=windows,
                )
            else:
                given = (gots[1 - role], outs[1 - role]) + ((objective,) if role else ())
                g2, g1 = call(
                    functools.partial(early_kernel, role, tick),
                    f"early_{role}_{tick}",
                    (table, pre1, pre2, taps, *given),
                    (FIELD, FIELD),
                    scratch=windows,
                )
            out = call(functools.partial(late_kernel, role), f"late_{role}_{tick}", (taps, g1), FIELD, scratch=windows)
            g2s.append(g2)
            g1s.append(g1)
            new_outs.append(out)
            new_gots.append(relay(out, role))
        gots, outs = new_gots, new_outs
        for role in range(2):
            for which, saved, fields, sums in ((1, pre1, g2s, sums2), (0, entries, g1s, sums1)):
                new = call(
                    functools.partial(wgrad_kernel, which, role, tick),
                    f"wgrad{which + 1}_{role}_{tick}",
                    (table, saved, fields[role], *sums[role]),
                    SUMS,
                    scratch=windows,
                    aliases={3: 0} if sums[role] else {},
                )
                sums[role] = (new,)

    part = jax.ShapeDtypeStruct((4, 2, 3, SHARE, CH), BF)
    staged = [pltpu.VMEM((9, CH, CH), F32)] * 2
    res = call(
        last_two_kernel,
        "last_two",
        (table, pre1, pre2, objective, gots[1], gots[0], *outs, *sums2[0], *sums2[1]),
        (part,) * 6 + (FIELD,) * 2,
        scratch=windows * 2 + staged,
        mib=16,
        ops=2,
    )
    keeps2, g2s = res[3:6], res[6:8]
    gots2 = [exchange(res[o], ORDERS[o][0]) for o in range(3)]
    g1s = [
        call(
            functools.partial(last_early_kernel, role),
            f"early_{role}_{TICKS - 1}",
            (table, pre1, taps, g2s[role]),
            FIELD,
            scratch=windows,
        )
        for role in range(2)
    ]
    res = call(
        last_one_kernel,
        "last_one",
        (table, entries, *g1s, *sums1[0], *sums1[1]),
        (part,) * 6,
        scratch=windows * 2 + staged,
        mib=16,
        ops=2,
    )
    keeps1 = res[3:6]
    gots1 = [exchange(res[o], ORDERS[o][0]) for o in range(3)]
    final = call(
        last_late_kernel,
        f"late_{TICKS - 1}",
        (taps, *g1s),
        jax.ShapeDtypeStruct((2, PIX, CH), BF),
        scratch=windows * 2,
        ops=2,
    )

    parts = []
    part2 = jax.ShapeDtypeStruct((2, 2, 2, 3, SHARE, CH), BF)
    part3 = jax.ShapeDtypeStruct((1, 2, 2, 3, SHARE, CH), BF)
    begun = call(fold_two_kernel, "fold_two", (*keeps2, *gots2), (part2,) * 6, ops=FOLD_COST)
    for o in range(3):
        send, keep = call(
            fold_one_kernel,
            f"fold_one_{o}",
            (keeps1[o], gots1[o], begun[o], begun[3 + o]),
            (part2, part2),
            aliases={2: 0, 3: 1},
        )
        got = exchange(send, ORDERS[o][1])
        send, keep = call(fold_in, f"fold_last_{o}", (keep, got), (part3, part3))
        parts += [keep, exchange(send, ORDERS[o][2])]
    scale = 1.0 / math.sqrt(TICKS * DP * PIX)
    grads = call(
        functools.partial(finish_kernel, scale),
        "finish",
        tuple(parts),
        jax.ShapeDtypeStruct((2, 2, 9, SHARE, CH), F32),
    )
    return (
        final.reshape(2, 1, 1, ROWS, COLS, CH),
        grads.reshape(2, 1, 2, 9, SHARE, CH),
    )


def solution(mesh):
    placed = (
        P(None, "section", "dp", None, None, None),
        P(None, "dp", None, None, None),
        P(None, "section", None, "dp", None, None, None),
        P(None, "section", None, "dp", None, None, None),
        P(None, "section", None, "dp", None, None, None),
        P(None, "section", None, None, None, None),
        P(),
    )
    return jax.shard_map(
        on_device,
        mesh=mesh,
        in_specs=placed,
        out_specs=(
            P(None, "section", "dp", None, None, None),
            P(None, "section", None, None, "dp", None),
        ),
        check_vma=False,
    )
```

```python
import functools
import math

import jax
import jax.numpy as jnp
from jax import lax
from jax.experimental import pallas as pl
from jax.experimental.pallas import tpu as pltpu
from jax.sharding import PartitionSpec as P

TICKS = 4
ROWS = 16
COLS = 32
PIX = ROWS * COLS
CH = 256
DP = 8
COST = 2 * 512 * 9 * 256 * 256
FOLD_COST = 16
PREPARE_MIB = 53
SHARE = CH // DP
BF = jnp.bfloat16
F32 = jnp.float32
NT = (((1,), (1,)), ((), ()))

PAIRS = {
    "a": [(d, (d & 4) + ((d & 3) ^ 1)) for d in range(DP)],
    "b": [(d, (d & 4) + 3 - (d & 3)) for d in range(DP)],
    "y": [(d, d ^ 4) for d in range(DP)],
}
ORDERS = ("aby", "bya", "yab")

VM = pl.BlockSpec(memory_space=pltpu.VMEM)
SM = pl.BlockSpec(memory_space=pltpu.SMEM)
HB = pl.BlockSpec(memory_space=pltpu.HBM)
FIELD = jax.ShapeDtypeStruct((PIX, CH), BF)
SUMS = jax.ShapeDtypeStruct((9, CH, CH), F32)
WINDOWS = pltpu.VMEM((3, PIX + 2 * COLS, CH), BF)


def half_of(role):
    odd = lax.axis_index("section") & 1
    return odd if role == 0 else 1 - odd


def call(kernel, name, given, outs, scratch=(), mib=8, aliases={}, ops=1, after=()):
    n_given = len(given)

    def body(*refs):
        kernel(*refs[:n_given], *refs[n_given + len(after) :])

    return pl.pallas_call(
        body if after else kernel,
        out_shape=outs,
        in_specs=[VM] * n_given + [pl.BlockSpec(memory_space=pl.ANY)] * len(after),
        out_specs=jax.tree.map(lambda _: VM, outs),
        scratch_shapes=list(scratch),
        input_output_aliases=aliases,
        compiler_params=pltpu.CompilerParams(vmem_limit_bytes=mib << 20),
        cost_estimate=pl.CostEstimate(flops=ops * COST, bytes_accessed=1024, transcendentals=0),
        name=name,
    )(*given, *after)


def clear_edges(win):
    edge = jnp.zeros((3, COLS, CH), BF)
    win[:, 0:COLS, :] = edge
    win[:, COLS + PIX : 2 * COLS + PIX, :] = edge


def fill_windows(win, field):
    clear_edges(win)
    col = lax.broadcasted_iota(jnp.int32, field.shape, 0) & (COLS - 1)
    win[0, COLS : COLS + PIX, :] = jnp.where(col == 0, 0.0, pltpu.roll(field, 1, 0)).astype(BF)
    win[1, COLS : COLS + PIX, :] = field.astype(BF)
    win[2, COLS : COLS + PIX, :] = jnp.where(col == COLS - 1, 0.0, pltpu.roll(field, PIX - 1, 0)).astype(BF)


def tap_of(win, k):
    dy, dx = divmod(k, 3)
    return win[dx, dy * COLS : dy * COLS + PIX, :]


def conv(win, taps, base):
    total = None
    for k in range(9):
        term = lax.dot_general(tap_of(win, k), taps[base + 8 - k], NT, preferred_element_type=F32)
        total = term if total is None else total + term
    return total


def slot_of(table, role, tick):
    half = half_of(role)
    column = half * lax.axis_size("section") + lax.axis_index("section")
    place = lax.broadcasted_iota(jnp.int32, table.shape, 1) == column
    row = lax.broadcasted_iota(jnp.int32, table.shape, 0) == tick
    return half * 4 + jnp.sum(jnp.where(place & row, table[...], 0))


def add_up(role, tick, got, other, objective):
    total = got[...].astype(F32)
    encoder = half_of(role) == 0
    total = total + jnp.where(encoder, other[...].astype(F32), 0.0)
    if role == 1:
        first = lax.axis_index("section") == 0
        total = jnp.where(first, objective[tick - 1].astype(F32), total)
    return total


def prepare_kernel(table, *refs):
    del table
    fields, laters, earlies = refs[0:2], refs[2:4], refs[4:6]
    g2s, masks = refs[6:8], refs[8:10]
    for role in range(2):
        g2s[role][...] = jnp.where(laters[role][0] > 0, fields[role][0], jnp.zeros((), BF))
        masks[role][...] = earlies[role][0]


def prepare(table, pending, pre1, pre2):
    def at_half(role, i, table):
        return half_of(role), 0, 0

    def at_slot(role, i, table):
        half = half_of(role)
        return 4 * half + table[0, half * lax.axis_size("section") + lax.axis_index("section")], 0, 0

    def blocks(place):
        return [pl.BlockSpec((1, PIX, CH), functools.partial(place, role)) for role in range(2)]

    return pl.pallas_call(
        prepare_kernel,
        grid_spec=pltpu.PrefetchScalarGridSpec(
            num_scalar_prefetch=1,
            grid=(1,),
            in_specs=blocks(at_half) + blocks(at_slot) + blocks(at_slot),
            out_specs=[VM] * 4,
        ),
        out_shape=[FIELD] * 4,
        compiler_params=pltpu.CompilerParams(vmem_limit_bytes=PREPARE_MIB << 20),
        cost_estimate=pl.CostEstimate(flops=1, bytes_accessed=1024, transcendentals=0),
        name="prepare",
    )(table, pending, pending, pre2, pre2, pre1, pre1)


def early_of_kernel(role, mask, taps, g2, g1_out, win):
    fill_windows(win, g2[...].astype(F32))
    g1_out[...] = jnp.where(mask[...] > 0, conv(win, taps, 18 * half_of(role) + 9), 0.0).astype(BF)


def early_kernel(role, tick, table, pre1, pre2, taps, *refs):
    given = refs[:-3]
    g2_out, g1_out, win = refs[-3:]
    slot = slot_of(table, role, tick)
    g2 = add_up(role, tick, *given, *([None] * (3 - len(given))))
    g2 = jnp.where(pre2[slot] > 0, g2, 0.0)
    g2_out[...] = g2.astype(BF)
    fill_windows(win, g2)
    g1_out[...] = jnp.where(pre1[slot] > 0, conv(win, taps, 18 * half_of(role) + 9), 0.0).astype(BF)


def late_kernel(role, taps, g1, out, win):
    fill_windows(win, g1[...].astype(F32))
    out[...] = conv(win, taps, 18 * half_of(role)).astype(BF)


def tap_grads(wins, xs, fields):
    for win, field in zip(wins, fields):
        fill_windows(win, field)
    xt = jnp.concatenate([x.T for x in xs], axis=1)
    for k in range(9):
        right = jnp.concatenate([tap_of(win, 8 - k) for win in wins], axis=0)
        yield k, jnp.dot(xt, right, preferred_element_type=F32)


def left_side(which, saved, slot):
    x = saved[slot]
    return jnp.maximum(x, jnp.zeros((), BF)) if which else x


def wgrad_kernel(which, role, table, saved, *refs):
    fields, new, wins = refs[:2], refs[2], refs[3:]
    xs = [left_side(which, saved, slot_of(table, role, tick)) for tick in range(2)]
    for k, term in tap_grads(wins, xs, [field[...].astype(F32) for field in fields]):
        new[k] = term


def replica_at(order, r):
    me = lax.axis_index("dp")
    bit = {order[i]: (r >> (2 - i)) & 1 for i in range(3)}
    y = (me >> 2) & 1
    z = me & 3
    beta = (z >> 1) & 1
    alpha = (z & 1) ^ beta
    alpha = alpha ^ bit["a"]
    beta = beta ^ bit["b"]
    return (y ^ bit["y"]) * 4 + 2 * beta + (alpha ^ beta)


def put_shares(staged, k, sends, keeps, role):
    o, at = divmod(k, 3)
    for r in range(DP):
        row = pl.multiple_of(replica_at(ORDERS[o], r) * SHARE, SHARE)
        share = staged[k, pl.ds(row, SHARE), :].astype(BF)
        if r >= 4:
            sends[o][r - 4, role, at] = share
        else:
            keeps[o][r, role, at] = share


def last_two_kernel(table, pre1, pre2, objective, *refs):
    given, befores, olds = refs[:4], refs[4:6], refs[6:8]
    sends, keeps, g2s = refs[8:11], refs[11:14], refs[14:16]
    wins, staged = refs[16:20], refs[20:22]
    tick = TICKS - 1
    for role in range(2):
        slot = slot_of(table, role, tick)
        g2 = add_up(role, tick, given[role], given[3 - role], objective)
        g2 = jnp.where(pre2[slot] > 0, g2, 0.0)
        g2s[role][...] = g2.astype(BF)
        xs = [left_side(1, pre1, slot_of(table, role, tick - 1)), left_side(1, pre1, slot)]
        fields = [befores[role][...].astype(F32), g2]
        for k, term in tap_grads(wins[2 * role : 2 * role + 2], xs, fields):
            staged[role][k] = olds[role][k] + term
            put_shares(staged[role], k, sends, keeps, role)


def last_early_kernel(role, table, pre1, taps, g2, g1_out, win):
    slot = slot_of(table, role, TICKS - 1)
    fill_windows(win, g2[...].astype(F32))
    g1_out[...] = jnp.where(pre1[slot] > 0, conv(win, taps, 18 * half_of(role) + 9), 0.0).astype(BF)


def last_one_kernel(table, entries, *refs):
    befores, g1s, olds = refs[:2], refs[2:4], refs[4:6]
    sends, keeps = refs[6:9], refs[9:12]
    wins, staged = refs[12:16], refs[16:18]
    for role in range(2):
        xs = [left_side(0, entries, slot_of(table, role, tick)) for tick in (TICKS - 2, TICKS - 1)]
        fields = [befores[role][...].astype(F32), g1s[role][...].astype(F32)]
        for k, term in tap_grads(wins[2 * role : 2 * role + 2], xs, fields):
            staged[role][k] = olds[role][k] + term
            put_shares(staged[role], k, sends, keeps, role)


def last_late_kernel(taps, g1_zero, g1_one, out, *wins):
    for role in range(2):
        half = half_of(role)
        fill_windows(wins[role], (g1_zero, g1_one)[role][...].astype(F32))
        out[half] = conv(wins[role], taps, 18 * half).astype(BF)


def fold_in(keep, got, send, left):
    half = keep.shape[0] // 2
    total = keep[...].astype(F32) + got[...].astype(F32)
    left[...] = total[:half].astype(BF)
    send[...] = total[half:].astype(BF)


def fold_two_kernel(*refs):
    for o in range(3):
        fold_in(*refs[o::3])


def fold_two_last_kernel(*refs):
    for o in range(3):
        keep, got, send, left = refs[o::3]
        fold_in(keep, got, send.at[:, 1], left.at[:, 1])


def fold_one_last_kernel(keep, got, old_send, old_left, send, left):
    del old_send, old_left
    fold_in(keep, got, send.at[:, 0], left.at[:, 0])


def finish_kernel(scale, *refs):
    out = refs[-1]
    for o in range(3):
        keep, got = refs[2 * o : 2 * o + 2]
        total = keep[0].astype(F32) + got[0].astype(F32)
        for role in range(2):
            half = half_of(role)
            for piece in range(2):
                out[half, piece, 3 * o : 3 * o + 3] = total[piece, role] * scale


def relay(block, role):
    levels = lax.axis_size("section")
    pairs = [(i, i + 1) for i in range(1 - role, levels - 1, 2)]
    return lax.ppermute(block, "section", pairs + [(b, a) for a, b in pairs])


def exchange(block, step):
    return lax.ppermute(block, "dp", PAIRS[step])


def on_device(
    pending_adjoints,
    objective_adjoints,
    kept_block_entries,
    kept_early_presums,
    kept_later_presums,
    filter_taps,
    slot_timetable,
):
    table = slot_timetable
    entries = kept_block_entries.reshape(8, PIX, CH)
    pre1 = kept_early_presums.reshape(8, PIX, CH)
    pre2 = kept_later_presums.reshape(8, PIX, CH)
    taps = filter_taps.reshape(36, CH, CH)
    pending = pending_adjoints.reshape(2, PIX, CH)
    objective = objective_adjoints.reshape(TICKS - 1, PIX, CH)
    windows = [WINDOWS]

    all_g2s, all_g1s = [], []

    def early_sums(which, saved, fields):
        return [
            call(
                functools.partial(wgrad_kernel, which, role),
                f"wgrad{which + 1}_{role}",
                (table, saved, fields[0][role], fields[1][role]),
                SUMS,
                scratch=windows * 2,
                ops=2,
            )
            for role in range(2)
        ]

    gots = outs = None
    prepared = prepare(table, pending, pre1, pre2)
    for tick in range(TICKS - 1):
        g2s, g1s, new_outs, new_gots = [], [], [], []
        for role in range(2):
            if tick == 0:
                g2, mask = prepared[role], prepared[2 + role]
                g1 = call(
                    functools.partial(early_of_kernel, role),
                    f"early_{role}_0",
                    (mask, taps, g2),
                    FIELD,
                    scratch=windows,
                )
            else:
                given = (gots[1 - role], outs[1 - role]) + ((objective,) if role else ())
                g2, g1 = call(
                    functools.partial(early_kernel, role, tick),
                    f"early_{role}_{tick}",
                    (table, pre1, pre2, taps, *given),
                    (FIELD, FIELD),
                    scratch=windows,
                    after=sums2 if tick == 2 else (),
                )
            out = call(functools.partial(late_kernel, role), f"late_{role}_{tick}", (taps, g1), FIELD, scratch=windows)
            g2s.append(g2)
            g1s.append(g1)
            new_outs.append(out)
            new_gots.append(relay(out, role))
        gots, outs = new_gots, new_outs
        all_g2s.append(g2s)
        all_g1s.append(g1s)
        if tick == 1:
            sums2 = early_sums(1, pre1, all_g2s)
            sums1 = early_sums(0, entries, all_g1s)

    part = jax.ShapeDtypeStruct((4, 2, 3, SHARE, CH), BF)
    staged = [pltpu.VMEM((9, CH, CH), F32)] * 2
    res = call(
        last_two_kernel,
        "last_two",
        (table, pre1, pre2, objective, gots[1], gots[0], *outs, *g2s, *sums2),
        (part,) * 6 + (FIELD,) * 2,
        scratch=windows * 4 + staged,
        mib=16,
        ops=4,
        after=sums1,
    )
    keeps2, g2s = res[3:6], res[6:8]
    gots2 = [exchange(res[o], ORDERS[o][0]) for o in range(3)]
    g1s = [
        call(
            functools.partial(last_early_kernel, role),
            f"early_{role}_{TICKS - 1}",
            (table, pre1, taps, g2s[role]),
            FIELD,
            scratch=windows,
        )
        for role in range(2)
    ]
    res = call(
        last_one_kernel,
        "last_one",
        (table, entries, *all_g1s[-1], *g1s, *sums1),
        (part,) * 6,
        scratch=windows * 4 + staged,
        mib=16,
        ops=4,
    )
    keeps1 = res[3:6]
    gots1 = [exchange(res[o], ORDERS[o][0]) for o in range(3)]
    final = call(
        last_late_kernel,
        f"late_{TICKS - 1}",
        (taps, *g1s),
        jax.ShapeDtypeStruct((2, PIX, CH), BF),
        scratch=windows * 2,
        ops=2,
    )

    parts = []
    part2 = jax.ShapeDtypeStruct((2, 2, 3, SHARE, CH), BF)
    part3 = jax.ShapeDtypeStruct((1, 2, 2, 3, SHARE, CH), BF)
    res = call(fold_two_kernel, "fold_two", (*keeps2, *gots2), (part2,) * 6, ops=FOLD_COST)
    gots2 = [exchange(res[o], ORDERS[o][1]) for o in range(3)]
    begun = call(fold_two_last_kernel, "fold_two_last", (*res[3:6], *gots2), (part3,) * 6, ops=FOLD_COST)
    for o in range(3):
        send, keep = call(fold_in, f"fold_one_{o}", (keeps1[o], gots1[o]), (part2, part2))
        got = exchange(send, ORDERS[o][1])
        send, keep = call(
            fold_one_last_kernel,
            f"fold_one_last_{o}",
            (keep, got, begun[o], begun[3 + o]),
            (part3, part3),
            aliases={2: 0, 3: 1},
        )
        parts += [keep, exchange(send, ORDERS[o][2])]
    scale = 1.0 / math.sqrt(TICKS * DP * PIX)
    grads = call(
        functools.partial(finish_kernel, scale),
        "finish",
        tuple(parts),
        jax.ShapeDtypeStruct((2, 2, 9, SHARE, CH), F32),
    )
    return (
        final.reshape(2, 1, 1, ROWS, COLS, CH),
        grads.reshape(2, 1, 2, 9, SHARE, CH),
    )


def solution(mesh):
    placed = (
        P(None, "section", "dp", None, None, None),
        P(None, "dp", None, None, None),
        P(None, "section", None, "dp", None, None, None),
        P(None, "section", None, "dp", None, None, None),
        P(None, "section", None, "dp", None, None, None),
        P(None, "section", None, None, None, None),
        P(),
    )
    return jax.shard_map(
        on_device,
        mesh=mesh,
        in_specs=placed,
        out_specs=(
            P(None, "section", "dp", None, None, None),
            P(None, "section", None, None, "dp", None),
        ),
        check_vma=False,
    )
```

```python
import functools
import math

import jax
import jax.numpy as jnp
from jax import lax
from jax.experimental import pallas as pl
from jax.experimental.pallas import tpu as pltpu
from jax.sharding import PartitionSpec as P

TICKS = 4
ROWS = 16
COLS = 32
PIX = ROWS * COLS
CH = 256
DP = 8
COST = 2 * 512 * 9 * 256 * 256
FOLD_COST = 16
PREPARE_KIB = 54016
SHARE = CH // DP
BF = jnp.bfloat16
F32 = jnp.float32
NT = (((1,), (1,)), ((), ()))

PAIRS = {
    "a": [(d, (d & 4) + ((d & 3) ^ 1)) for d in range(DP)],
    "b": [(d, (d & 4) + 3 - (d & 3)) for d in range(DP)],
    "y": [(d, d ^ 4) for d in range(DP)],
}
ORDERS = ("aby", "bya", "yab")

VM = pl.BlockSpec(memory_space=pltpu.VMEM)
SM = pl.BlockSpec(memory_space=pltpu.SMEM)
HB = pl.BlockSpec(memory_space=pltpu.HBM)
FIELD = jax.ShapeDtypeStruct((PIX, CH), BF)
SUMS = jax.ShapeDtypeStruct((9, CH, CH), F32)
WINDOWS = pltpu.VMEM((3, PIX + 2 * COLS, CH), BF)


def half_of(role):
    odd = lax.axis_index("section") & 1
    return odd if role == 0 else 1 - odd


def call(kernel, name, given, outs, scratch=(), mib=8, aliases={}, ops=1, after=()):
    n_given = len(given)

    def body(*refs):
        kernel(*refs[:n_given], *refs[n_given + len(after) :])

    return pl.pallas_call(
        body if after else kernel,
        out_shape=outs,
        in_specs=[VM] * n_given + [pl.BlockSpec(memory_space=pl.ANY)] * len(after),
        out_specs=jax.tree.map(lambda _: VM, outs),
        scratch_shapes=list(scratch),
        input_output_aliases=aliases,
        compiler_params=pltpu.CompilerParams(vmem_limit_bytes=mib << 20),
        cost_estimate=pl.CostEstimate(flops=ops * COST, bytes_accessed=1024, transcendentals=0),
        name=name,
    )(*given, *after)


def clear_edges(win):
    edge = jnp.zeros((3, COLS, CH), BF)
    win[:, 0:COLS, :] = edge
    win[:, COLS + PIX : 2 * COLS + PIX, :] = edge


def fill_windows(win, field):
    clear_edges(win)
    col = lax.broadcasted_iota(jnp.int32, field.shape, 0) & (COLS - 1)
    win[0, COLS : COLS + PIX, :] = jnp.where(col == 0, 0.0, pltpu.roll(field, 1, 0)).astype(BF)
    win[1, COLS : COLS + PIX, :] = field.astype(BF)
    win[2, COLS : COLS + PIX, :] = jnp.where(col == COLS - 1, 0.0, pltpu.roll(field, PIX - 1, 0)).astype(BF)


def tap_of(win, k):
    dy, dx = divmod(k, 3)
    return win[dx, dy * COLS : dy * COLS + PIX, :]


def conv(win, taps, base):
    total = None
    for k in range(9):
        term = lax.dot_general(tap_of(win, k), taps[base + 8 - k], NT, preferred_element_type=F32)
        total = term if total is None else total + term
    return total


def slot_of(table, role, tick):
    half = half_of(role)
    column = half * lax.axis_size("section") + lax.axis_index("section")
    place = lax.broadcasted_iota(jnp.int32, table.shape, 1) == column
    row = lax.broadcasted_iota(jnp.int32, table.shape, 0) == tick
    return half * 4 + jnp.sum(jnp.where(place & row, table[...], 0))


def add_up(role, tick, got, other, objective):
    total = got[...].astype(F32)
    encoder = half_of(role) == 0
    total = total + jnp.where(encoder, other[...].astype(F32), 0.0)
    if role == 1:
        first = lax.axis_index("section") == 0
        total = jnp.where(first, objective[tick - 1].astype(F32), total)
    return total


def prepare_kernel(table, *refs):
    del table
    fields, laters, earlies = refs[0:2], refs[2:4], refs[4:6]
    g2s, masks = refs[6:8], refs[8:10]
    for role in range(2):
        g2s[role][...] = jnp.where(laters[role][0] > 0, fields[role][0], jnp.zeros((), BF))
        masks[role][...] = earlies[role][0]


def prepare(table, pending, pre1, pre2):
    def at_half(role, i, table):
        return half_of(role), 0, 0

    def at_slot(role, i, table):
        half = half_of(role)
        return 4 * half + table[0, half * lax.axis_size("section") + lax.axis_index("section")], 0, 0

    def blocks(place):
        return [pl.BlockSpec((1, PIX, CH), functools.partial(place, role)) for role in range(2)]

    return pl.pallas_call(
        prepare_kernel,
        grid_spec=pltpu.PrefetchScalarGridSpec(
            num_scalar_prefetch=1,
            grid=(1,),
            in_specs=blocks(at_half) + blocks(at_slot) + blocks(at_slot),
            out_specs=[VM] * 4,
        ),
        out_shape=[FIELD] * 4,
        compiler_params=pltpu.CompilerParams(vmem_limit_bytes=PREPARE_KIB << 10),
        cost_estimate=pl.CostEstimate(flops=1, bytes_accessed=1024, transcendentals=0),
        name="prepare",
    )(table, pending, pending, pre2, pre2, pre1, pre1)


def early_of_kernel(role, mask, taps, g2, g1_out, win):
    fill_windows(win, g2[...].astype(F32))
    g1_out[...] = jnp.where(mask[...] > 0, conv(win, taps, 18 * half_of(role) + 9), 0.0).astype(BF)


def early_kernel(role, tick, table, pre1, pre2, taps, *refs):
    given = refs[:-3]
    g2_out, g1_out, win = refs[-3:]
    slot = slot_of(table, role, tick)
    g2 = add_up(role, tick, *given, *([None] * (3 - len(given))))
    g2 = jnp.where(pre2[slot] > 0, g2, 0.0)
    g2_out[...] = g2.astype(BF)
    fill_windows(win, g2)
    g1_out[...] = jnp.where(pre1[slot] > 0, conv(win, taps, 18 * half_of(role) + 9), 0.0).astype(BF)


def late_kernel(role, taps, g1, out, win):
    fill_windows(win, g1[...].astype(F32))
    out[...] = conv(win, taps, 18 * half_of(role)).astype(BF)


def tap_grads(wins, xs, fields):
    for win, field in zip(wins, fields):
        fill_windows(win, field)
    xt = jnp.concatenate([x.T for x in xs], axis=1)
    for k in range(9):
        right = jnp.concatenate([tap_of(win, 8 - k) for win in wins], axis=0)
        yield k, jnp.dot(xt, right, preferred_element_type=F32)


def left_side(which, saved, slot):
    x = saved[slot]
    return jnp.maximum(x, jnp.zeros((), BF)) if which else x


def wgrad_kernel(which, role, table, saved, *refs):
    ticks = len(refs) // 2
    fields, new, wins = refs[:ticks], refs[ticks], refs[ticks + 1 :]
    xs = [left_side(which, saved, slot_of(table, role, tick)) for tick in range(ticks)]
    for k, term in tap_grads(wins, xs, [field[...].astype(F32) for field in fields]):
        new[k] = term


def replica_at(order, r):
    me = lax.axis_index("dp")
    bit = {order[i]: (r >> (2 - i)) & 1 for i in range(3)}
    y = (me >> 2) & 1
    z = me & 3
    beta = (z >> 1) & 1
    alpha = (z & 1) ^ beta
    alpha = alpha ^ bit["a"]
    beta = beta ^ bit["b"]
    return (y ^ bit["y"]) * 4 + 2 * beta + (alpha ^ beta)


def put_shares(staged, k, sends, keeps, role):
    o, at = divmod(k, 3)
    for r in range(DP):
        row = pl.multiple_of(replica_at(ORDERS[o], r) * SHARE, SHARE)
        share = staged[k, pl.ds(row, SHARE), :].astype(BF)
        if r >= 4:
            sends[o][r - 4, role, at] = share
        else:
            keeps[o][r, role, at] = share


def last_two_kernel(table, pre1, pre2, objective, *refs):
    given, olds = refs[:4], refs[4:6]
    sends, keeps, g2s = refs[6:9], refs[9:12], refs[12:14]
    wins, staged = refs[14:16], refs[16:18]
    tick = TICKS - 1
    for role in range(2):
        slot = slot_of(table, role, tick)
        g2 = add_up(role, tick, given[role], given[3 - role], objective)
        g2 = jnp.where(pre2[slot] > 0, g2, 0.0)
        g2s[role][...] = g2.astype(BF)
        for k, term in tap_grads(wins[role : role + 1], [left_side(1, pre1, slot)], [g2]):
            staged[role][k] = olds[role][k] + term
            put_shares(staged[role], k, sends, keeps, role)


def last_early_kernel(role, table, pre1, taps, g2, g1_out, win):
    slot = slot_of(table, role, TICKS - 1)
    fill_windows(win, g2[...].astype(F32))
    g1_out[...] = jnp.where(pre1[slot] > 0, conv(win, taps, 18 * half_of(role) + 9), 0.0).astype(BF)


def last_one_kernel(table, entries, *refs):
    befores, g1s, olds = refs[:2], refs[2:4], refs[4:6]
    sends, keeps = refs[6:9], refs[9:12]
    wins, staged = refs[12:16], refs[16:18]
    for role in range(2):
        xs = [left_side(0, entries, slot_of(table, role, tick)) for tick in (TICKS - 2, TICKS - 1)]
        fields = [befores[role][...].astype(F32), g1s[role][...].astype(F32)]
        for k, term in tap_grads(wins[2 * role : 2 * role + 2], xs, fields):
            staged[role][k] = olds[role][k] + term
            put_shares(staged[role], k, sends, keeps, role)


def last_late_kernel(taps, g1_zero, g1_one, out, *wins):
    for role in range(2):
        half = half_of(role)
        fill_windows(wins[role], (g1_zero, g1_one)[role][...].astype(F32))
        out[half] = conv(wins[role], taps, 18 * half).astype(BF)


def fold_in(keep, got, send, left):
    half = keep.shape[0] // 2
    total = keep[...].astype(F32) + got[...].astype(F32)
    left[...] = total[:half].astype(BF)
    send[...] = total[half:].astype(BF)


def fold_kernel(*refs):
    for o in range(3):
        fold_in(*refs[o::3])


def fold_two_last_kernel(*refs):
    for o in range(3):
        keep, got, send, left = refs[o::3]
        fold_in(keep, got, send.at[:, 1], left.at[:, 1])


def fold_one_last_kernel(keep, got, old_send, old_left, send, left):
    del old_send, old_left
    fold_in(keep, got, send.at[:, 0], left.at[:, 0])


def finish_kernel(scale, *refs):
    out = refs[-1]
    for o in range(3):
        keep, got = refs[2 * o : 2 * o + 2]
        total = keep[0].astype(F32) + got[0].astype(F32)
        for role in range(2):
            half = half_of(role)
            for piece in range(2):
                out[half, piece, 3 * o : 3 * o + 3] = total[piece, role] * scale


def relay(block, role):
    levels = lax.axis_size("section")
    pairs = [(i, i + 1) for i in range(1 - role, levels - 1, 2)]
    return lax.ppermute(block, "section", pairs + [(b, a) for a, b in pairs])


def exchange(block, step):
    return lax.ppermute(block, "dp", PAIRS[step])


def on_device(
    pending_adjoints,
    objective_adjoints,
    kept_block_entries,
    kept_early_presums,
    kept_later_presums,
    filter_taps,
    slot_timetable,
):
    table = slot_timetable
    entries = kept_block_entries.reshape(8, PIX, CH)
    pre1 = kept_early_presums.reshape(8, PIX, CH)
    pre2 = kept_later_presums.reshape(8, PIX, CH)
    taps = filter_taps.reshape(36, CH, CH)
    pending = pending_adjoints.reshape(2, PIX, CH)
    objective = objective_adjoints.reshape(TICKS - 1, PIX, CH)
    windows = [WINDOWS]

    all_g2s, all_g1s = [], []

    def early_sums(which, saved, fields):
        return [
            call(
                functools.partial(wgrad_kernel, which, role),
                f"wgrad{which + 1}_{role}",
                (table, saved, *[field[role] for field in fields]),
                SUMS,
                scratch=windows * len(fields),
                mib=12,
                ops=len(fields),
            )
            for role in range(2)
        ]

    gots = outs = None
    prepared = prepare(table, pending, pre1, pre2)
    for tick in range(TICKS - 1):
        g2s, g1s, new_outs, new_gots = [], [], [], []
        for role in range(2):
            if tick == 0:
                g2, mask = prepared[role], prepared[2 + role]
                g1 = call(
                    functools.partial(early_of_kernel, role),
                    f"early_{role}_0",
                    (mask, taps, g2),
                    FIELD,
                    scratch=windows,
                )
            else:
                given = (gots[1 - role], outs[1 - role]) + ((objective,) if role else ())
                g2, g1 = call(
                    functools.partial(early_kernel, role, tick),
                    f"early_{role}_{tick}",
                    (table, pre1, pre2, taps, *given),
                    (FIELD, FIELD),
                    scratch=windows,
                    after=sums1 if tick == 2 else (),
                )
            out = call(functools.partial(late_kernel, role), f"late_{role}_{tick}", (taps, g1), FIELD, scratch=windows)
            g2s.append(g2)
            g1s.append(g1)
            new_outs.append(out)
            new_gots.append(relay(out, role))
        gots, outs = new_gots, new_outs
        all_g2s.append(g2s)
        all_g1s.append(g1s)
        if tick == 1:
            sums1 = early_sums(0, entries, all_g1s)
    sums2 = early_sums(1, pre1, all_g2s)

    part = jax.ShapeDtypeStruct((4, 2, 3, SHARE, CH), BF)
    staged = [pltpu.VMEM((9, CH, CH), F32)] * 2
    res = call(
        last_two_kernel,
        "last_two",
        (table, pre1, pre2, objective, gots[1], gots[0], *outs, *sums2),
        (part,) * 6 + (FIELD,) * 2,
        scratch=windows * 2 + staged,
        mib=16,
        ops=2,
    )
    keeps2, g2s = res[3:6], res[6:8]
    gots2 = [exchange(res[o], ORDERS[o][0]) for o in range(3)]
    g1s = [
        call(
            functools.partial(last_early_kernel, role),
            f"early_{role}_{TICKS - 1}",
            (table, pre1, taps, g2s[role]),
            FIELD,
            scratch=windows,
        )
        for role in range(2)
    ]
    res = call(
        last_one_kernel,
        "last_one",
        (table, entries, *all_g1s[-1], *g1s, *sums1),
        (part,) * 6,
        scratch=windows * 4 + staged,
        mib=16,
        ops=4,
    )
    keeps1 = res[3:6]
    gots1 = [exchange(res[o], ORDERS[o][0]) for o in range(3)]
    final = call(
        last_late_kernel,
        f"late_{TICKS - 1}",
        (taps, *g1s),
        jax.ShapeDtypeStruct((2, PIX, CH), BF),
        scratch=windows * 2,
        ops=2,
    )

    parts = []
    part2 = jax.ShapeDtypeStruct((2, 2, 3, SHARE, CH), BF)
    part3 = jax.ShapeDtypeStruct((1, 2, 2, 3, SHARE, CH), BF)
    res = call(fold_kernel, "fold_two", (*keeps2, *gots2), (part2,) * 6, ops=FOLD_COST)
    gots2 = [exchange(res[o], ORDERS[o][1]) for o in range(3)]
    begun = call(fold_two_last_kernel, "fold_two_last", (*res[3:6], *gots2), (part3,) * 6, ops=FOLD_COST)
    for o in range(3):
        send, keep = call(fold_in, f"fold_one_{o}", (keeps1[o], gots1[o]), (part2, part2))
        got = exchange(send, ORDERS[o][1])
        send, keep = call(
            fold_one_last_kernel,
            f"fold_one_last_{o}",
            (keep, got, begun[o], begun[3 + o]),
            (part3, part3),
            aliases={2: 0, 3: 1},
        )
        parts += [keep, exchange(send, ORDERS[o][2])]
    scale = 1.0 / math.sqrt(TICKS * DP * PIX)
    grads = call(
        functools.partial(finish_kernel, scale),
        "finish",
        tuple(parts),
        jax.ShapeDtypeStruct((2, 2, 9, SHARE, CH), F32),
    )
    return (
        final.reshape(2, 1, 1, ROWS, COLS, CH),
        grads.reshape(2, 1, 2, 9, SHARE, CH),
    )


def solution(mesh):
    placed = (
        P(None, "section", "dp", None, None, None),
        P(None, "dp", None, None, None),
        P(None, "section", None, "dp", None, None, None),
        P(None, "section", None, "dp", None, None, None),
        P(None, "section", None, "dp", None, None, None),
        P(None, "section", None, None, None, None),
        P(),
    )
    return jax.shard_map(
        on_device,
        mesh=mesh,
        in_specs=placed,
        out_specs=(
            P(None, "section", "dp", None, None, None),
            P(None, "section", None, None, "dp", None),
        ),
        check_vma=False,
    )
```

```python
import functools
import math

import jax
import jax.numpy as jnp
from jax import lax
from jax.experimental import pallas as pl
from jax.experimental.pallas import tpu as pltpu
from jax.sharding import PartitionSpec as P

TICKS = 4
ROWS = 16
COLS = 32
PIX = ROWS * COLS
CH = 256
DP = 8
COST = 2 * 512 * 9 * 256 * 256
FOLD_COST = 16
PREPARE_KIB = 54016
SHARE = CH // DP
BF = jnp.bfloat16
F32 = jnp.float32
NT = (((1,), (1,)), ((), ()))

PAIRS = {
    "a": [(d, (d & 4) + ((d & 3) ^ 1)) for d in range(DP)],
    "b": [(d, (d & 4) + 3 - (d & 3)) for d in range(DP)],
    "y": [(d, d ^ 4) for d in range(DP)],
}
ORDERS = ("aby", "bya", "yab")

VM = pl.BlockSpec(memory_space=pltpu.VMEM)
SM = pl.BlockSpec(memory_space=pltpu.SMEM)
HB = pl.BlockSpec(memory_space=pltpu.HBM)
FIELD = jax.ShapeDtypeStruct((PIX, CH), BF)
SUMS = jax.ShapeDtypeStruct((9, CH, CH), F32)
WINDOWS = pltpu.VMEM((3, PIX + 2 * COLS, CH), BF)


def half_of(role):
    odd = lax.axis_index("section") & 1
    return odd if role == 0 else 1 - odd


def call(kernel, name, given, outs, scratch=(), mib=8, aliases={}, ops=1, after=()):
    n_given = len(given)

    def body(*refs):
        kernel(*refs[:n_given], *refs[n_given + len(after) :])

    return pl.pallas_call(
        body if after else kernel,
        out_shape=outs,
        in_specs=[VM] * n_given + [pl.BlockSpec(memory_space=pl.ANY)] * len(after),
        out_specs=jax.tree.map(lambda _: VM, outs),
        scratch_shapes=list(scratch),
        input_output_aliases=aliases,
        compiler_params=pltpu.CompilerParams(vmem_limit_bytes=mib << 20),
        cost_estimate=pl.CostEstimate(flops=ops * COST, bytes_accessed=1024, transcendentals=0),
        name=name,
    )(*given, *after)


def clear_edges(win):
    edge = jnp.zeros((3, COLS, CH), BF)
    win[:, 0:COLS, :] = edge
    win[:, COLS + PIX : 2 * COLS + PIX, :] = edge


def fill_windows(win, field):
    clear_edges(win)
    col = lax.broadcasted_iota(jnp.int32, field.shape, 0) & (COLS - 1)
    win[0, COLS : COLS + PIX, :] = jnp.where(col == 0, 0.0, pltpu.roll(field, 1, 0)).astype(BF)
    win[1, COLS : COLS + PIX, :] = field.astype(BF)
    win[2, COLS : COLS + PIX, :] = jnp.where(col == COLS - 1, 0.0, pltpu.roll(field, PIX - 1, 0)).astype(BF)


def tap_of(win, k):
    dy, dx = divmod(k, 3)
    return win[dx, dy * COLS : dy * COLS + PIX, :]


def conv(win, taps, base):
    total = None
    for k in range(9):
        term = lax.dot_general(tap_of(win, k), taps[base + 8 - k], NT, preferred_element_type=F32)
        total = term if total is None else total + term
    return total


def slot_of(table, role, tick):
    half = half_of(role)
    column = half * lax.axis_size("section") + lax.axis_index("section")
    place = lax.broadcasted_iota(jnp.int32, table.shape, 1) == column
    row = lax.broadcasted_iota(jnp.int32, table.shape, 0) == tick
    return half * 4 + jnp.sum(jnp.where(place & row, table[...], 0))


def add_up(role, tick, got, other, objective):
    total = got[...].astype(F32)
    encoder = half_of(role) == 0
    total = total + jnp.where(encoder, other[...].astype(F32), 0.0)
    if role == 1:
        first = lax.axis_index("section") == 0
        total = jnp.where(first, objective[tick - 1].astype(F32), total)
    return total


def prepare_kernel(table, *refs):
    del table
    fields, laters, earlies = refs[0:2], refs[2:4], refs[4:6]
    g2s, masks = refs[6:8], refs[8:10]
    for role in range(2):
        g2s[role][...] = jnp.where(laters[role][0] > 0, fields[role][0], jnp.zeros((), BF))
        masks[role][...] = earlies[role][0]


def prepare(table, pending, pre1, pre2):
    def at_half(role, i, table):
        return half_of(role), 0, 0

    def at_slot(role, i, table):
        half = half_of(role)
        return 4 * half + table[0, half * lax.axis_size("section") + lax.axis_index("section")], 0, 0

    def blocks(place):
        return [pl.BlockSpec((1, PIX, CH), functools.partial(place, role)) for role in range(2)]

    return pl.pallas_call(
        prepare_kernel,
        grid_spec=pltpu.PrefetchScalarGridSpec(
            num_scalar_prefetch=1,
            grid=(1,),
            in_specs=blocks(at_half) + blocks(at_slot) + blocks(at_slot),
            out_specs=[VM] * 4,
        ),
        out_shape=[FIELD] * 4,
        compiler_params=pltpu.CompilerParams(vmem_limit_bytes=PREPARE_KIB << 10),
        cost_estimate=pl.CostEstimate(flops=1, bytes_accessed=1024, transcendentals=0),
        name="prepare",
    )(table, pending, pending, pre2, pre2, pre1, pre1)


def early_of_kernel(role, mask, taps, g2, g1_out, win):
    fill_windows(win, g2[...].astype(F32))
    g1_out[...] = jnp.where(mask[...] > 0, conv(win, taps, 18 * half_of(role) + 9), 0.0).astype(BF)


def early_kernel(role, tick, table, pre1, pre2, taps, *refs):
    given = refs[:-3]
    g2_out, g1_out, win = refs[-3:]
    slot = slot_of(table, role, tick)
    g2 = add_up(role, tick, *given, *([None] * (3 - len(given))))
    g2 = jnp.where(pre2[slot] > 0, g2, 0.0)
    g2_out[...] = g2.astype(BF)
    fill_windows(win, g2)
    g1_out[...] = jnp.where(pre1[slot] > 0, conv(win, taps, 18 * half_of(role) + 9), 0.0).astype(BF)


def late_kernel(role, taps, g1, out, win):
    fill_windows(win, g1[...].astype(F32))
    out[...] = conv(win, taps, 18 * half_of(role)).astype(BF)


def tap_grads(wins, xs, fields):
    for win, field in zip(wins, fields):
        fill_windows(win, field)
    xt = jnp.concatenate([x.T for x in xs], axis=1)
    for k in range(9):
        right = jnp.concatenate([tap_of(win, 8 - k) for win in wins], axis=0)
        yield k, jnp.dot(xt, right, preferred_element_type=F32)


def left_side(which, saved, slot):
    x = saved[slot]
    return jnp.maximum(x, jnp.zeros((), BF)) if which else x


def wgrad_kernel(which, role, table, saved, *refs):
    ticks = len(refs) // 2
    fields, new, wins = refs[:ticks], refs[ticks], refs[ticks + 1 :]
    xs = [left_side(which, saved, slot_of(table, role, tick)) for tick in range(ticks)]
    for k, term in tap_grads(wins, xs, [field[...].astype(F32) for field in fields]):
        new[k] = term


def replica_at(order, r):
    me = lax.axis_index("dp")
    bit = {order[i]: (r >> (2 - i)) & 1 for i in range(3)}
    y = (me >> 2) & 1
    z = me & 3
    beta = (z >> 1) & 1
    alpha = (z & 1) ^ beta
    alpha = alpha ^ bit["a"]
    beta = beta ^ bit["b"]
    return (y ^ bit["y"]) * 4 + 2 * beta + (alpha ^ beta)


def put_shares(staged, k, sends, keeps, role):
    o, at = divmod(k, 3)
    for r in range(DP):
        row = pl.multiple_of(replica_at(ORDERS[o], r) * SHARE, SHARE)
        share = staged[k, pl.ds(row, SHARE), :].astype(BF)
        if r >= 4:
            sends[o][r - 4, role, at] = share
        else:
            keeps[o][r, role, at] = share


def last_two_kernel(table, pre1, pre2, objective, *refs):
    given, olds = refs[:4], refs[4:6]
    sends, keeps, g2s = refs[6:9], refs[9:12], refs[12:14]
    wins, staged = refs[14:16], refs[16:18]
    tick = TICKS - 1
    for role in range(2):
        slot = slot_of(table, role, tick)
        g2 = add_up(role, tick, given[role], given[3 - role], objective)
        g2 = jnp.where(pre2[slot] > 0, g2, 0.0)
        g2s[role][...] = g2.astype(BF)
        for k, term in tap_grads(wins[role : role + 1], [left_side(1, pre1, slot)], [g2]):
            staged[role][k] = olds[role][k] + term
            put_shares(staged[role], k, sends, keeps, role)


def last_early_kernel(role, table, pre1, taps, g2, g1_out, win):
    slot = slot_of(table, role, TICKS - 1)
    fill_windows(win, g2[...].astype(F32))
    g1_out[...] = jnp.where(pre1[slot] > 0, conv(win, taps, 18 * half_of(role) + 9), 0.0).astype(BF)


def last_one_kernel(table, entries, *refs):
    befores, g1s, olds = refs[:2], refs[2:4], refs[4:6]
    sends, keeps = refs[6:9], refs[9:12]
    wins, staged = refs[12:16], refs[16:18]
    for role in range(2):
        xs = [left_side(0, entries, slot_of(table, role, tick)) for tick in (TICKS - 2, TICKS - 1)]
        fields = [befores[role][...].astype(F32), g1s[role][...].astype(F32)]
        for k, term in tap_grads(wins[2 * role : 2 * role + 2], xs, fields):
            staged[role][k] = olds[role][k] + term
            put_shares(staged[role], k, sends, keeps, role)


def last_late_kernel(taps, g1_zero, g1_one, out, *wins):
    for role in range(2):
        half = half_of(role)
        fill_windows(wins[role], (g1_zero, g1_one)[role][...].astype(F32))
        out[half] = conv(wins[role], taps, 18 * half).astype(BF)


def fold_in(keep, got, send, left):
    half = keep.shape[0] // 2
    total = keep[...].astype(F32) + got[...].astype(F32)
    left[...] = total[:half].astype(BF)
    send[...] = total[half:].astype(BF)


def fold_kernel(*refs):
    for o in range(3):
        fold_in(*refs[o::3])


def fold_two_last_kernel(*refs):
    for o in range(3):
        keep, got, send, left = refs[o::3]
        fold_in(keep, got, send.at[:, 1], left.at[:, 1])


def fold_one_last_kernel(keep, got, old_send, old_left, send, left):
    del old_send, old_left
    fold_in(keep, got, send.at[:, 0], left.at[:, 0])


def finish_some_kernel(scale, *refs):
    out = refs[-1]
    for o in range(2):
        keep, got = refs[2 * o : 2 * o + 2]
        total = keep[0].astype(F32) + got[0].astype(F32)
        for role in range(2):
            for piece in range(2):
                out[half_of(role), piece, 3 * o : 3 * o + 3] = total[piece, role] * scale


def finish_kernel(scale, some, keep, got, out):
    out[:, :, 0:6] = some[...]
    total = keep[0].astype(F32) + got[0].astype(F32)
    for role in range(2):
        for piece in range(2):
            out[half_of(role), piece, 6:9] = total[piece, role] * scale


def relay(block, role):
    levels = lax.axis_size("section")
    pairs = [(i, i + 1) for i in range(1 - role, levels - 1, 2)]
    return lax.ppermute(block, "section", pairs + [(b, a) for a, b in pairs])


def exchange(block, step):
    return lax.ppermute(block, "dp", PAIRS[step])


def on_device(
    pending_adjoints,
    objective_adjoints,
    kept_block_entries,
    kept_early_presums,
    kept_later_presums,
    filter_taps,
    slot_timetable,
):
    table = slot_timetable
    entries = kept_block_entries.reshape(8, PIX, CH)
    pre1 = kept_early_presums.reshape(8, PIX, CH)
    pre2 = kept_later_presums.reshape(8, PIX, CH)
    taps = filter_taps.reshape(36, CH, CH)
    pending = pending_adjoints.reshape(2, PIX, CH)
    objective = objective_adjoints.reshape(TICKS - 1, PIX, CH)
    windows = [WINDOWS]

    all_g2s, all_g1s = [], []

    def early_sums(which, saved, fields):
        return [
            call(
                functools.partial(wgrad_kernel, which, role),
                f"wgrad{which + 1}_{role}",
                (table, saved, *[field[role] for field in fields]),
                SUMS,
                scratch=windows * len(fields),
                mib=12,
                ops=len(fields),
            )
            for role in range(2)
        ]

    gots = outs = None
    prepared = prepare(table, pending, pre1, pre2)
    for tick in range(TICKS - 1):
        g2s, g1s, new_outs, new_gots = [], [], [], []
        for role in range(2):
            if tick == 0:
                g2, mask = prepared[role], prepared[2 + role]
                g1 = call(
                    functools.partial(early_of_kernel, role),
                    f"early_{role}_0",
                    (mask, taps, g2),
                    FIELD,
                    scratch=windows,
                )
            else:
                given = (gots[1 - role], outs[1 - role]) + ((objective,) if role else ())
                g2, g1 = call(
                    functools.partial(early_kernel, role, tick),
                    f"early_{role}_{tick}",
                    (table, pre1, pre2, taps, *given),
                    (FIELD, FIELD),
                    scratch=windows,
                    after=sums1 if tick == 2 else (),
                )
            out = call(functools.partial(late_kernel, role), f"late_{role}_{tick}", (taps, g1), FIELD, scratch=windows)
            g2s.append(g2)
            g1s.append(g1)
            new_outs.append(out)
            new_gots.append(relay(out, role))
        gots, outs = new_gots, new_outs
        all_g2s.append(g2s)
        all_g1s.append(g1s)
        if tick == 1:
            sums1 = early_sums(0, entries, all_g1s)
    sums2 = early_sums(1, pre1, all_g2s)

    part = jax.ShapeDtypeStruct((4, 2, 3, SHARE, CH), BF)
    staged = [pltpu.VMEM((9, CH, CH), F32)] * 2
    res = call(
        last_two_kernel,
        "last_two",
        (table, pre1, pre2, objective, gots[1], gots[0], *outs, *sums2),
        (part,) * 6 + (FIELD,) * 2,
        scratch=windows * 2 + staged,
        mib=16,
        ops=2,
    )
    keeps2, g2s = res[3:6], res[6:8]
    gots2 = [exchange(res[o], ORDERS[o][0]) for o in range(3)]
    g1s = [
        call(
            functools.partial(last_early_kernel, role),
            f"early_{role}_{TICKS - 1}",
            (table, pre1, taps, g2s[role]),
            FIELD,
            scratch=windows,
        )
        for role in range(2)
    ]
    res = call(
        last_one_kernel,
        "last_one",
        (table, entries, *all_g1s[-1], *g1s, *sums1),
        (part,) * 6,
        scratch=windows * 4 + staged,
        mib=16,
        ops=4,
    )
    keeps1 = res[3:6]
    gots1 = [exchange(res[o], ORDERS[o][0]) for o in range(3)]
    final = call(
        last_late_kernel,
        f"late_{TICKS - 1}",
        (taps, *g1s),
        jax.ShapeDtypeStruct((2, PIX, CH), BF),
        scratch=windows * 2,
        ops=2,
    )

    parts = []
    part2 = jax.ShapeDtypeStruct((2, 2, 3, SHARE, CH), BF)
    part3 = jax.ShapeDtypeStruct((1, 2, 2, 3, SHARE, CH), BF)
    res = call(fold_kernel, "fold_two", (*keeps2, *gots2), (part2,) * 6, ops=FOLD_COST)
    gots2 = [exchange(res[o], ORDERS[o][1]) for o in range(3)]
    begun = call(fold_two_last_kernel, "fold_two_last", (*res[3:6], *gots2), (part3,) * 6, ops=FOLD_COST)
    firsts = []
    for o in range(3):
        send, keep = call(fold_in, f"fold_one_{o}", (keeps1[o], gots1[o]), (part2, part2), after=firsts[-1:])
        firsts.append(keep)
        gots1[o] = exchange(send, ORDERS[o][1])
    lasts = []
    for o in range(3):
        send, keep = call(
            fold_one_last_kernel,
            f"fold_one_last_{o}",
            (firsts[o], gots1[o], begun[o], begun[3 + o]),
            (part3, part3),
            aliases={2: 0, 3: 1},
            after=lasts[-1:],
        )
        lasts.append(keep)
        parts += [keep, exchange(send, ORDERS[o][2])]
    scale = 1.0 / math.sqrt(TICKS * DP * PIX)
    some = call(
        functools.partial(finish_some_kernel, scale),
        "finish_some",
        tuple(parts[:4]),
        jax.ShapeDtypeStruct((2, 2, 6, SHARE, CH), F32),
        ops=FOLD_COST,
    )
    grads = call(
        functools.partial(finish_kernel, scale),
        "finish",
        (some, *parts[4:]),
        jax.ShapeDtypeStruct((2, 2, 9, SHARE, CH), F32),
    )
    return (
        final.reshape(2, 1, 1, ROWS, COLS, CH),
        grads.reshape(2, 1, 2, 9, SHARE, CH),
    )


def solution(mesh):
    placed = (
        P(None, "section", "dp", None, None, None),
        P(None, "dp", None, None, None),
        P(None, "section", None, "dp", None, None, None),
        P(None, "section", None, "dp", None, None, None),
        P(None, "section", None, "dp", None, None, None),
        P(None, "section", None, None, None, None),
        P(),
    )
    return jax.shard_map(
        on_device,
        mesh=mesh,
        in_specs=placed,
        out_specs=(
            P(None, "section", "dp", None, None, None),
            P(None, "section", None, None, "dp", None),
        ),
        check_vma=False,
    )
```

```python
import functools
import math

import jax
import jax.numpy as jnp
from jax import lax
from jax.experimental import pallas as pl
from jax.experimental.pallas import tpu as pltpu
from jax.sharding import PartitionSpec as P

TICKS = 4
ROWS = 16
COLS = 32
PIX = ROWS * COLS
CH = 256
DP = 8
COST = 2 * 512 * 9 * 256 * 256
FOLD_COST = 16
PREPARE_KIB = 54016
SHARE = CH // DP
BF = jnp.bfloat16
F32 = jnp.float32
NT = (((1,), (1,)), ((), ()))

PAIRS = {
    "a": [(d, (d & 4) + ((d & 3) ^ 1)) for d in range(DP)],
    "b": [(d, (d & 4) + 3 - (d & 3)) for d in range(DP)],
    "y": [(d, d ^ 4) for d in range(DP)],
}
ORDERS = ("aby", "bya", "yab")

VM = pl.BlockSpec(memory_space=pltpu.VMEM)
SM = pl.BlockSpec(memory_space=pltpu.SMEM)
HB = pl.BlockSpec(memory_space=pltpu.HBM)
FIELD = jax.ShapeDtypeStruct((PIX, CH), BF)
MARK = jax.ShapeDtypeStruct((8, 128), F32)
SUMS = jax.ShapeDtypeStruct((9, CH, CH), F32)
WINDOWS = pltpu.VMEM((3, PIX + 2 * COLS, CH), BF)


def half_of(role):
    odd = lax.axis_index("section") & 1
    return odd if role == 0 else 1 - odd


def call(kernel, name, given, outs, scratch=(), mib=8, aliases={}, ops=1, after=()):
    n_given = len(given)

    def body(*refs):
        kernel(*refs[:n_given], *refs[n_given + len(after) :])

    return pl.pallas_call(
        body if after else kernel,
        out_shape=outs,
        in_specs=[VM] * n_given + [pl.BlockSpec(memory_space=pl.ANY)] * len(after),
        out_specs=jax.tree.map(lambda _: VM, outs),
        scratch_shapes=list(scratch),
        input_output_aliases=aliases,
        compiler_params=pltpu.CompilerParams(vmem_limit_bytes=mib << 20),
        cost_estimate=pl.CostEstimate(flops=ops * COST, bytes_accessed=1024, transcendentals=0),
        name=name,
    )(*given, *after)


def clear_edges(win):
    edge = jnp.zeros((3, COLS, CH), BF)
    win[:, 0:COLS, :] = edge
    win[:, COLS + PIX : 2 * COLS + PIX, :] = edge


def fill_windows(win, field):
    clear_edges(win)
    col = lax.broadcasted_iota(jnp.int32, field.shape, 0) & (COLS - 1)
    win[0, COLS : COLS + PIX, :] = jnp.where(col == 0, 0.0, pltpu.roll(field, 1, 0)).astype(BF)
    win[1, COLS : COLS + PIX, :] = field.astype(BF)
    win[2, COLS : COLS + PIX, :] = jnp.where(col == COLS - 1, 0.0, pltpu.roll(field, PIX - 1, 0)).astype(BF)


def tap_of(win, k):
    dy, dx = divmod(k, 3)
    return win[dx, dy * COLS : dy * COLS + PIX, :]


def conv(win, taps, base):
    total = None
    for k in range(9):
        term = lax.dot_general(tap_of(win, k), taps[base + 8 - k], NT, preferred_element_type=F32)
        total = term if total is None else total + term
    return total


def slot_of(table, role, tick):
    half = half_of(role)
    column = half * lax.axis_size("section") + lax.axis_index("section")
    place = lax.broadcasted_iota(jnp.int32, table.shape, 1) == column
    row = lax.broadcasted_iota(jnp.int32, table.shape, 0) == tick
    return half * 4 + jnp.sum(jnp.where(place & row, table[...], 0))


def add_up(role, tick, got, other, objective):
    total = got[...].astype(F32)
    encoder = half_of(role) == 0
    total = total + jnp.where(encoder, other[...].astype(F32), 0.0)
    if role == 1:
        first = lax.axis_index("section") == 0
        total = jnp.where(first, objective[tick - 1].astype(F32), total)
    return total


def prepare_kernel(table, *refs):
    del table
    fields, laters, earlies = refs[0:2], refs[2:4], refs[4:6]
    g2s, masks = refs[6:8], refs[8:10]
    for role in range(2):
        g2s[role][...] = jnp.where(laters[role][0] > 0, fields[role][0], jnp.zeros((), BF))
        masks[role][...] = earlies[role][0]


def prepare(table, pending, pre1, pre2):
    def at_half(role, i, table):
        return half_of(role), 0, 0

    def at_slot(role, i, table):
        half = half_of(role)
        return 4 * half + table[0, half * lax.axis_size("section") + lax.axis_index("section")], 0, 0

    def blocks(place):
        return [pl.BlockSpec((1, PIX, CH), functools.partial(place, role)) for role in range(2)]

    return pl.pallas_call(
        prepare_kernel,
        grid_spec=pltpu.PrefetchScalarGridSpec(
            num_scalar_prefetch=1,
            grid=(1,),
            in_specs=blocks(at_half) + blocks(at_slot) + blocks(at_slot),
            out_specs=[VM] * 4,
        ),
        out_shape=[FIELD] * 4,
        compiler_params=pltpu.CompilerParams(vmem_limit_bytes=PREPARE_KIB << 10),
        cost_estimate=pl.CostEstimate(flops=1, bytes_accessed=1024, transcendentals=0),
        name="prepare",
    )(table, pending, pending, pre2, pre2, pre1, pre1)


def early_of_kernel(role, mask, taps, g2, g1_out, win):
    fill_windows(win, g2[...].astype(F32))
    g1_out[...] = jnp.where(mask[...] > 0, conv(win, taps, 18 * half_of(role) + 9), 0.0).astype(BF)


def early_kernel(role, tick, table, pre1, pre2, taps, *refs):
    given = refs[:-3]
    g2_out, g1_out, win = refs[-3:]
    slot = slot_of(table, role, tick)
    g2 = add_up(role, tick, *given, *([None] * (3 - len(given))))
    g2 = jnp.where(pre2[slot] > 0, g2, 0.0)
    g2_out[...] = g2.astype(BF)
    fill_windows(win, g2)
    g1_out[...] = jnp.where(pre1[slot] > 0, conv(win, taps, 18 * half_of(role) + 9), 0.0).astype(BF)


def late_kernel(role, taps, g1, out, win):
    fill_windows(win, g1[...].astype(F32))
    out[...] = conv(win, taps, 18 * half_of(role)).astype(BF)


def tap_grads(wins, xs, fields):
    for win, field in zip(wins, fields):
        fill_windows(win, field)
    xt = jnp.concatenate([x.T for x in xs], axis=1)
    for k in range(9):
        right = jnp.concatenate([tap_of(win, 8 - k) for win in wins], axis=0)
        yield k, jnp.dot(xt, right, preferred_element_type=F32)


def left_side(which, saved, slot):
    x = saved[slot]
    return jnp.maximum(x, jnp.zeros((), BF)) if which else x


def wgrad_kernel(which, role, table, saved, *refs):
    ticks = len(refs) // 2
    fields, new, wins = refs[:ticks], refs[ticks], refs[ticks + 1 :]
    xs = [left_side(which, saved, slot_of(table, role, tick)) for tick in range(ticks)]
    for k, term in tap_grads(wins, xs, [field[...].astype(F32) for field in fields]):
        new[k] = term


def replica_at(order, r):
    me = lax.axis_index("dp")
    bit = {order[i]: (r >> (2 - i)) & 1 for i in range(3)}
    y = (me >> 2) & 1
    z = me & 3
    beta = (z >> 1) & 1
    alpha = (z & 1) ^ beta
    alpha = alpha ^ bit["a"]
    beta = beta ^ bit["b"]
    return (y ^ bit["y"]) * 4 + 2 * beta + (alpha ^ beta)


def put_shares(staged, k, sends, keeps, role):
    o, at = divmod(k, 3)
    for r in range(DP):
        row = pl.multiple_of(replica_at(ORDERS[o], r) * SHARE, SHARE)
        share = staged[k, pl.ds(row, SHARE), :].astype(BF)
        if r >= 4:
            sends[o][r - 4, role, at] = share
        else:
            keeps[o][r, role, at] = share


def last_two_kernel(table, pre1, pre2, objective, *refs):
    given, olds = refs[:4], refs[4:6]
    sends, keeps, g2s = refs[6:9], refs[9:12], refs[12:14]
    wins, staged = refs[14:16], refs[16:18]
    tick = TICKS - 1
    for role in range(2):
        slot = slot_of(table, role, tick)
        g2 = add_up(role, tick, given[role], given[3 - role], objective)
        g2 = jnp.where(pre2[slot] > 0, g2, 0.0)
        g2s[role][...] = g2.astype(BF)
        for k, term in tap_grads(wins[role : role + 1], [left_side(1, pre1, slot)], [g2]):
            staged[role][k] = olds[role][k] + term
            put_shares(staged[role], k, sends, keeps, role)


def last_early_kernel(role, table, pre1, taps, g2, g1_out, win):
    slot = slot_of(table, role, TICKS - 1)
    fill_windows(win, g2[...].astype(F32))
    g1_out[...] = jnp.where(pre1[slot] > 0, conv(win, taps, 18 * half_of(role) + 9), 0.0).astype(BF)


def last_one_kernel(table, entries, *refs):
    befores, g1s, olds = refs[:2], refs[2:4], refs[4:6]
    sends, keeps = refs[6:9], refs[9:12]
    wins, staged = refs[12:16], refs[16:18]
    for role in range(2):
        xs = [left_side(0, entries, slot_of(table, role, tick)) for tick in (TICKS - 2, TICKS - 1)]
        fields = [befores[role][...].astype(F32), g1s[role][...].astype(F32)]
        for k, term in tap_grads(wins[2 * role : 2 * role + 2], xs, fields):
            staged[role][k] = olds[role][k] + term
            put_shares(staged[role], k, sends, keeps, role)


def last_late_kernel(taps, g1_zero, g1_one, out, mark, *wins):
    mark[...] = jnp.zeros(MARK.shape, F32)
    for role in range(2):
        half = half_of(role)
        fill_windows(wins[role], (g1_zero, g1_one)[role][...].astype(F32))
        out[half] = conv(wins[role], taps, 18 * half).astype(BF)


def fold_in(keep, got, send, left):
    half = keep.shape[0] // 2
    total = keep[...].astype(F32) + got[...].astype(F32)
    left[...] = total[:half].astype(BF)
    send[...] = total[half:].astype(BF)


def fold_kernel(*refs):
    for o in range(3):
        fold_in(*refs[o::3])


def fold_two_last_kernel(*refs):
    for o in range(3):
        keep, got, send, left = refs[o::3]
        fold_in(keep, got, send.at[:, 1], left.at[:, 1])


def fold_one_last_kernel(keep, got, old_send, old_left, send, left):
    del old_send, old_left
    fold_in(keep, got, send.at[:, 0], left.at[:, 0])


def finish_some_kernel(scale, *refs):
    out = refs[-1]
    for o in range(2):
        keep, got = refs[2 * o : 2 * o + 2]
        total = keep[0].astype(F32) + got[0].astype(F32)
        for role in range(2):
            for piece in range(2):
                out[half_of(role), piece, 3 * o : 3 * o + 3] = total[piece, role] * scale


def finish_kernel(scale, some, keep, got, out):
    out[:, :, 0:6] = some[...]
    total = keep[0].astype(F32) + got[0].astype(F32)
    for role in range(2):
        for piece in range(2):
            out[half_of(role), piece, 6:9] = total[piece, role] * scale


def relay(block, role):
    levels = lax.axis_size("section")
    pairs = [(i, i + 1) for i in range(1 - role, levels - 1, 2)]
    return lax.ppermute(block, "section", pairs + [(b, a) for a, b in pairs])


def exchange(block, step):
    return lax.ppermute(block, "dp", PAIRS[step])


def on_device(
    pending_adjoints,
    objective_adjoints,
    kept_block_entries,
    kept_early_presums,
    kept_later_presums,
    filter_taps,
    slot_timetable,
):
    table = slot_timetable
    entries = kept_block_entries.reshape(8, PIX, CH)
    pre1 = kept_early_presums.reshape(8, PIX, CH)
    pre2 = kept_later_presums.reshape(8, PIX, CH)
    taps = filter_taps.reshape(36, CH, CH)
    pending = pending_adjoints.reshape(2, PIX, CH)
    objective = objective_adjoints.reshape(TICKS - 1, PIX, CH)
    windows = [WINDOWS]

    all_g2s, all_g1s = [], []

    def early_sums(which, saved, fields):
        return [
            call(
                functools.partial(wgrad_kernel, which, role),
                f"wgrad{which + 1}_{role}",
                (table, saved, *[field[role] for field in fields]),
                SUMS,
                scratch=windows * len(fields),
                mib=12,
                ops=len(fields),
            )
            for role in range(2)
        ]

    gots = outs = None
    prepared = prepare(table, pending, pre1, pre2)
    for tick in range(TICKS - 1):
        g2s, g1s, new_outs, new_gots = [], [], [], []
        for role in range(2):
            if tick == 0:
                g2, mask = prepared[role], prepared[2 + role]
                g1 = call(
                    functools.partial(early_of_kernel, role),
                    f"early_{role}_0",
                    (mask, taps, g2),
                    FIELD,
                    scratch=windows,
                )
            else:
                given = (gots[1 - role], outs[1 - role]) + ((objective,) if role else ())
                g2, g1 = call(
                    functools.partial(early_kernel, role, tick),
                    f"early_{role}_{tick}",
                    (table, pre1, pre2, taps, *given),
                    (FIELD, FIELD),
                    scratch=windows,
                    after=sums1 if tick == 2 else (),
                )
            out = call(functools.partial(late_kernel, role), f"late_{role}_{tick}", (taps, g1), FIELD, scratch=windows)
            g2s.append(g2)
            g1s.append(g1)
            new_outs.append(out)
            new_gots.append(relay(out, role))
        gots, outs = new_gots, new_outs
        all_g2s.append(g2s)
        all_g1s.append(g1s)
        if tick == 1:
            sums1 = early_sums(0, entries, all_g1s)
    sums2 = early_sums(1, pre1, all_g2s)

    part = jax.ShapeDtypeStruct((4, 2, 3, SHARE, CH), BF)
    staged = [pltpu.VMEM((9, CH, CH), F32)] * 2
    res = call(
        last_two_kernel,
        "last_two",
        (table, pre1, pre2, objective, gots[1], gots[0], *outs, *sums2),
        (part,) * 6 + (FIELD,) * 2,
        scratch=windows * 2 + staged,
        mib=16,
        ops=2,
    )
    keeps2, g2s = res[3:6], res[6:8]
    gots2 = [exchange(res[o], ORDERS[o][0]) for o in range(3)]
    g1s = [
        call(
            functools.partial(last_early_kernel, role),
            f"early_{role}_{TICKS - 1}",
            (table, pre1, taps, g2s[role]),
            FIELD,
            scratch=windows,
        )
        for role in range(2)
    ]
    res = call(
        last_one_kernel,
        "last_one",
        (table, entries, *all_g1s[-1], *g1s, *sums1),
        (part,) * 6,
        scratch=windows * 4 + staged,
        mib=16,
        ops=4,
    )
    keeps1 = res[3:6]
    gots1 = [exchange(res[o], ORDERS[o][0]) for o in range(3)]
    final, mark = call(
        last_late_kernel,
        f"late_{TICKS - 1}",
        (taps, *g1s),
        (jax.ShapeDtypeStruct((2, PIX, CH), BF), MARK),
        scratch=windows * 2,
        ops=2,
    )

    parts = []
    part2 = jax.ShapeDtypeStruct((2, 2, 3, SHARE, CH), BF)
    part3 = jax.ShapeDtypeStruct((1, 2, 2, 3, SHARE, CH), BF)
    res = call(fold_kernel, "fold_two", (*keeps2, *gots2), (part2,) * 6, ops=FOLD_COST)
    gots2 = [exchange(res[o], ORDERS[o][1]) for o in range(3)]
    begun = call(fold_two_last_kernel, "fold_two_last", (*res[3:6], *gots2), (part3,) * 6, ops=FOLD_COST)
    firsts = []
    order = [mark]
    for o in range(3):
        send, keep = call(fold_in, f"fold_one_{o}", (keeps1[o], gots1[o]), (part2, part2), after=order[-1:])
        firsts.append(keep)
        order.append(keep)
        gots1[o] = exchange(send, ORDERS[o][1])
    lasts = []
    for o in range(3):
        send, keep = call(
            fold_one_last_kernel,
            f"fold_one_last_{o}",
            (firsts[o], gots1[o], begun[o], begun[3 + o]),
            (part3, part3),
            aliases={2: 0, 3: 1},
            after=lasts[-1:],
        )
        lasts.append(keep)
        parts += [keep, exchange(send, ORDERS[o][2])]
    scale = 1.0 / math.sqrt(TICKS * DP * PIX)
    some = call(
        functools.partial(finish_some_kernel, scale),
        "finish_some",
        tuple(parts[:4]),
        jax.ShapeDtypeStruct((2, 2, 6, SHARE, CH), F32),
        ops=FOLD_COST,
    )
    grads = call(
        functools.partial(finish_kernel, scale),
        "finish",
        (some, *parts[4:]),
        jax.ShapeDtypeStruct((2, 2, 9, SHARE, CH), F32),
    )
    return (
        final.reshape(2, 1, 1, ROWS, COLS, CH),
        grads.reshape(2, 1, 2, 9, SHARE, CH),
    )


def solution(mesh):
    placed = (
        P(None, "section", "dp", None, None, None),
        P(None, "dp", None, None, None),
        P(None, "section", None, "dp", None, None, None),
        P(None, "section", None, "dp", None, None, None),
        P(None, "section", None, "dp", None, None, None),
        P(None, "section", None, None, None, None),
        P(),
    )
    return jax.shard_map(
        on_device,
        mesh=mesh,
        in_specs=placed,
        out_specs=(
            P(None, "section", "dp", None, None, None),
            P(None, "section", None, None, "dp", None),
        ),
        check_vma=False,
    )
```

```python
import functools
import math

import jax
import jax.numpy as jnp
from jax import lax
from jax.experimental import pallas as pl
from jax.experimental.pallas import tpu as pltpu
from jax.sharding import PartitionSpec as P

TICKS = 4
ROWS = 16
COLS = 32
PIX = ROWS * COLS
CH = 256
DP = 8
COST = 2 * 512 * 9 * 256 * 256
FOLD_COST = 16
PREPARE_KIB = 54016
SHARE = CH // DP
BF = jnp.bfloat16
F32 = jnp.float32
NT = (((1,), (1,)), ((), ()))

PAIRS = {
    "a": [(d, (d & 4) + ((d & 3) ^ 1)) for d in range(DP)],
    "b": [(d, (d & 4) + 3 - (d & 3)) for d in range(DP)],
    "y": [(d, d ^ 4) for d in range(DP)],
}
ORDERS = ("aby", "bya", "yab")
TAPS = ((2, 2, 5), (5, 4, 0))
FIRST = tuple(tuple(sum(taps[:o]) for o in range(3)) for taps in TAPS)

VM = pl.BlockSpec(memory_space=pltpu.VMEM)
SM = pl.BlockSpec(memory_space=pltpu.SMEM)
HB = pl.BlockSpec(memory_space=pltpu.HBM)
FIELD = jax.ShapeDtypeStruct((PIX, CH), BF)
MARK = jax.ShapeDtypeStruct((8, 128), F32)
SUMS = jax.ShapeDtypeStruct((9, CH, CH), F32)
WINDOWS = pltpu.VMEM((3, PIX + 2 * COLS, CH), BF)


def half_of(role):
    odd = lax.axis_index("section") & 1
    return odd if role == 0 else 1 - odd


def call(kernel, name, given, outs, scratch=(), mib=8, aliases={}, ops=1, after=()):
    n_given = len(given)

    def body(*refs):
        kernel(*refs[:n_given], *refs[n_given + len(after) :])

    return pl.pallas_call(
        body if after else kernel,
        out_shape=outs,
        in_specs=[VM] * n_given + [pl.BlockSpec(memory_space=pl.ANY)] * len(after),
        out_specs=jax.tree.map(lambda _: VM, outs),
        scratch_shapes=list(scratch),
        input_output_aliases=aliases,
        compiler_params=pltpu.CompilerParams(vmem_limit_bytes=mib << 20),
        cost_estimate=pl.CostEstimate(flops=ops * COST, bytes_accessed=1024, transcendentals=0),
        name=name,
    )(*given, *after)


def clear_edges(win):
    edge = jnp.zeros((3, COLS, CH), BF)
    win[:, 0:COLS, :] = edge
    win[:, COLS + PIX : 2 * COLS + PIX, :] = edge


def fill_windows(win, field):
    clear_edges(win)
    col = lax.broadcasted_iota(jnp.int32, field.shape, 0) & (COLS - 1)
    win[0, COLS : COLS + PIX, :] = jnp.where(col == 0, 0.0, pltpu.roll(field, 1, 0)).astype(BF)
    win[1, COLS : COLS + PIX, :] = field.astype(BF)
    win[2, COLS : COLS + PIX, :] = jnp.where(col == COLS - 1, 0.0, pltpu.roll(field, PIX - 1, 0)).astype(BF)


def tap_of(win, k):
    dy, dx = divmod(k, 3)
    return win[dx, dy * COLS : dy * COLS + PIX, :]


def conv(win, taps, base):
    total = None
    for k in range(9):
        term = lax.dot_general(tap_of(win, k), taps[base + 8 - k], NT, preferred_element_type=F32)
        total = term if total is None else total + term
    return total


def slot_of(table, role, tick):
    half = half_of(role)
    column = half * lax.axis_size("section") + lax.axis_index("section")
    place = lax.broadcasted_iota(jnp.int32, table.shape, 1) == column
    row = lax.broadcasted_iota(jnp.int32, table.shape, 0) == tick
    return half * 4 + jnp.sum(jnp.where(place & row, table[...], 0))


def add_up(role, tick, got, other, objective):
    total = got[...].astype(F32)
    encoder = half_of(role) == 0
    total = total + jnp.where(encoder, other[...].astype(F32), 0.0)
    if role == 1:
        first = lax.axis_index("section") == 0
        total = jnp.where(first, objective[tick - 1].astype(F32), total)
    return total


def prepare_kernel(table, *refs):
    del table
    fields, laters, earlies = refs[0:2], refs[2:4], refs[4:6]
    g2s, masks = refs[6:8], refs[8:10]
    for role in range(2):
        g2s[role][...] = jnp.where(laters[role][0] > 0, fields[role][0], jnp.zeros((), BF))
        masks[role][...] = earlies[role][0]


def prepare(table, pending, pre1, pre2):
    def at_half(role, i, table):
        return half_of(role), 0, 0

    def at_slot(role, i, table):
        half = half_of(role)
        return 4 * half + table[0, half * lax.axis_size("section") + lax.axis_index("section")], 0, 0

    def blocks(place):
        return [pl.BlockSpec((1, PIX, CH), functools.partial(place, role)) for role in range(2)]

    return pl.pallas_call(
        prepare_kernel,
        grid_spec=pltpu.PrefetchScalarGridSpec(
            num_scalar_prefetch=1,
            grid=(1,),
            in_specs=blocks(at_half) + blocks(at_slot) + blocks(at_slot),
            out_specs=[VM] * 4,
        ),
        out_shape=[FIELD] * 4,
        compiler_params=pltpu.CompilerParams(vmem_limit_bytes=PREPARE_KIB << 10),
        cost_estimate=pl.CostEstimate(flops=1, bytes_accessed=1024, transcendentals=0),
        name="prepare",
    )(table, pending, pending, pre2, pre2, pre1, pre1)


def early_of_kernel(role, mask, taps, g2, g1_out, win):
    fill_windows(win, g2[...].astype(F32))
    g1_out[...] = jnp.where(mask[...] > 0, conv(win, taps, 18 * half_of(role) + 9), 0.0).astype(BF)


def early_kernel(role, tick, table, pre1, pre2, taps, *refs):
    given = refs[:-3]
    g2_out, g1_out, win = refs[-3:]
    slot = slot_of(table, role, tick)
    g2 = add_up(role, tick, *given, *([None] * (3 - len(given))))
    g2 = jnp.where(pre2[slot] > 0, g2, 0.0)
    g2_out[...] = g2.astype(BF)
    fill_windows(win, g2)
    g1_out[...] = jnp.where(pre1[slot] > 0, conv(win, taps, 18 * half_of(role) + 9), 0.0).astype(BF)


def late_kernel(role, taps, g1, out, win):
    fill_windows(win, g1[...].astype(F32))
    out[...] = conv(win, taps, 18 * half_of(role)).astype(BF)


def tap_grads(wins, xs, fields):
    for win, field in zip(wins, fields):
        fill_windows(win, field)
    xt = jnp.concatenate([x.T for x in xs], axis=1)
    for k in range(9):
        right = jnp.concatenate([tap_of(win, 8 - k) for win in wins], axis=0)
        yield k, jnp.dot(xt, right, preferred_element_type=F32)


def left_side(which, saved, slot):
    x = saved[slot]
    return jnp.maximum(x, jnp.zeros((), BF)) if which else x


def wgrad_kernel(which, role, table, saved, *refs):
    ticks = len(refs) // 2
    fields, new, wins = refs[:ticks], refs[ticks], refs[ticks + 1 :]
    xs = [left_side(which, saved, slot_of(table, role, tick)) for tick in range(ticks)]
    for k, term in tap_grads(wins, xs, [field[...].astype(F32) for field in fields]):
        new[k] = term


def replica_at(order, r):
    me = lax.axis_index("dp")
    bit = {order[i]: (r >> (2 - i)) & 1 for i in range(3)}
    y = (me >> 2) & 1
    z = me & 3
    beta = (z >> 1) & 1
    alpha = (z & 1) ^ beta
    alpha = alpha ^ bit["a"]
    beta = beta ^ bit["b"]
    return (y ^ bit["y"]) * 4 + 2 * beta + (alpha ^ beta)


def put_shares(staged, piece, k, sends, keeps, role):
    o = sum(k >= first for first in FIRST[piece][1:])
    at = k - FIRST[piece][o]
    for r in range(DP):
        row = pl.multiple_of(replica_at(ORDERS[o], r) * SHARE, SHARE)
        share = staged[k, pl.ds(row, SHARE), :].astype(BF)
        if r >= 4:
            sends[o][r - 4, role, at] = share
        else:
            keeps[o][r, role, at] = share


def last_two_kernel(table, pre1, pre2, objective, *refs):
    given, olds = refs[:4], refs[4:6]
    sends, keeps, g2s = refs[6:8], refs[8:10], refs[10:12]
    wins, staged = refs[12:14], refs[14:16]
    tick = TICKS - 1
    for role in range(2):
        slot = slot_of(table, role, tick)
        g2 = add_up(role, tick, given[role], given[3 - role], objective)
        g2 = jnp.where(pre2[slot] > 0, g2, 0.0)
        g2s[role][...] = g2.astype(BF)
        for k, term in tap_grads(wins[role : role + 1], [left_side(1, pre1, slot)], [g2]):
            staged[role][k] = olds[role][k] + term
            put_shares(staged[role], 1, k, sends, keeps, role)


def last_early_kernel(role, table, pre1, taps, g2, g1_out, win):
    slot = slot_of(table, role, TICKS - 1)
    fill_windows(win, g2[...].astype(F32))
    g1_out[...] = jnp.where(pre1[slot] > 0, conv(win, taps, 18 * half_of(role) + 9), 0.0).astype(BF)


def last_one_kernel(table, entries, *refs):
    befores, g1s, olds = refs[:2], refs[2:4], refs[4:6]
    sends, keeps = refs[6:9], refs[9:12]
    wins, staged = refs[12:16], refs[16:18]
    for role in range(2):
        xs = [left_side(0, entries, slot_of(table, role, tick)) for tick in (TICKS - 2, TICKS - 1)]
        fields = [befores[role][...].astype(F32), g1s[role][...].astype(F32)]
        for k, term in tap_grads(wins[2 * role : 2 * role + 2], xs, fields):
            staged[role][k] = olds[role][k] + term
            put_shares(staged[role], 0, k, sends, keeps, role)


def last_late_kernel(taps, g1_zero, g1_one, out, mark, *wins):
    mark[...] = jnp.zeros(MARK.shape, F32)
    for role in range(2):
        half = half_of(role)
        fill_windows(wins[role], (g1_zero, g1_one)[role][...].astype(F32))
        out[half] = conv(wins[role], taps, 18 * half).astype(BF)


def fold_in(keep, got, send, left):
    half = keep.shape[0] // 2
    total = keep[...].astype(F32) + got[...].astype(F32)
    left[...] = total[:half].astype(BF)
    send[...] = total[half:].astype(BF)


def fold_two_kernel(*refs):
    for o in range(2):
        fold_in(*refs[o::2])


def fold_two_last_kernel(*refs):
    for o in range(2):
        keep, got, send, left = refs[o::2]
        fold_in(keep, got, send.at[:, :, TAPS[0][o] :], left.at[:, :, TAPS[0][o] :])


def fold_one_last_kernel(o, *refs):
    keep, got = refs[:2]
    send, left = refs[-2:]
    fold_in(keep, got, send.at[:, :, : TAPS[0][o]], left.at[:, :, : TAPS[0][o]])


def finish_order(scale, o, keep, got, out):
    total = keep[0].astype(F32) + got[0].astype(F32)
    for role in range(2):
        for piece in range(2):
            taps, first = TAPS[piece][o], FIRST[piece][o]
            if taps:
                low = TAPS[0][o] * piece
                out[half_of(role), piece, first : first + taps] = total[role, low : low + taps] * scale


def finish_some_kernel(scale, *refs):
    for o in range(2):
        finish_order(scale, o, *refs[2 * o : 2 * o + 2], refs[-1])


def finish_kernel(scale, some, keep, got, out):
    for piece in range(2):
        first = FIRST[piece][2]
        out[:, piece, 0:first] = some[:, piece, 0:first]
    finish_order(scale, 2, keep, got, out)


def relay(block, role):
    levels = lax.axis_size("section")
    pairs = [(i, i + 1) for i in range(1 - role, levels - 1, 2)]
    return lax.ppermute(block, "section", pairs + [(b, a) for a, b in pairs])


def exchange(block, step):
    return lax.ppermute(block, "dp", PAIRS[step])


def on_device(
    pending_adjoints,
    objective_adjoints,
    kept_block_entries,
    kept_early_presums,
    kept_later_presums,
    filter_taps,
    slot_timetable,
):
    table = slot_timetable
    entries = kept_block_entries.reshape(8, PIX, CH)
    pre1 = kept_early_presums.reshape(8, PIX, CH)
    pre2 = kept_later_presums.reshape(8, PIX, CH)
    taps = filter_taps.reshape(36, CH, CH)
    pending = pending_adjoints.reshape(2, PIX, CH)
    objective = objective_adjoints.reshape(TICKS - 1, PIX, CH)
    windows = [WINDOWS]

    all_g2s, all_g1s = [], []

    def early_sums(which, saved, fields):
        return [
            call(
                functools.partial(wgrad_kernel, which, role),
                f"wgrad{which + 1}_{role}",
                (table, saved, *[field[role] for field in fields]),
                SUMS,
                scratch=windows * len(fields),
                mib=12,
                ops=len(fields),
            )
            for role in range(2)
        ]

    gots = outs = None
    prepared = prepare(table, pending, pre1, pre2)
    for tick in range(TICKS - 1):
        g2s, g1s, new_outs, new_gots = [], [], [], []
        for role in range(2):
            if tick == 0:
                g2, mask = prepared[role], prepared[2 + role]
                g1 = call(
                    functools.partial(early_of_kernel, role),
                    f"early_{role}_0",
                    (mask, taps, g2),
                    FIELD,
                    scratch=windows,
                )
            else:
                given = (gots[1 - role], outs[1 - role]) + ((objective,) if role else ())
                g2, g1 = call(
                    functools.partial(early_kernel, role, tick),
                    f"early_{role}_{tick}",
                    (table, pre1, pre2, taps, *given),
                    (FIELD, FIELD),
                    scratch=windows,
                    after=sums1 if tick == 2 else (),
                )
            out = call(functools.partial(late_kernel, role), f"late_{role}_{tick}", (taps, g1), FIELD, scratch=windows)
            g2s.append(g2)
            g1s.append(g1)
            new_outs.append(out)
            new_gots.append(relay(out, role))
        gots, outs = new_gots, new_outs
        all_g2s.append(g2s)
        all_g1s.append(g1s)
        if tick == 1:
            sums1 = early_sums(0, entries, all_g1s)
    sums2 = early_sums(1, pre1, all_g2s)

    def part(chunks, taps):
        return jax.ShapeDtypeStruct((chunks, 2, taps, SHARE, CH), BF)

    staged = [pltpu.VMEM((9, CH, CH), F32)] * 2
    res = call(
        last_two_kernel,
        "last_two",
        (table, pre1, pre2, objective, gots[1], gots[0], *outs, *sums2),
        tuple(part(4, taps) for taps in TAPS[1][:2] * 2) + (FIELD,) * 2,
        scratch=windows * 2 + staged,
        mib=16,
        ops=2,
    )
    keeps2, g2s = res[2:4], res[4:6]
    gots2 = [exchange(res[o], ORDERS[o][0]) for o in range(2)]
    g1s = [
        call(
            functools.partial(last_early_kernel, role),
            f"early_{role}_{TICKS - 1}",
            (table, pre1, taps, g2s[role]),
            FIELD,
            scratch=windows,
        )
        for role in range(2)
    ]
    res = call(
        last_one_kernel,
        "last_one",
        (table, entries, *all_g1s[-1], *g1s, *sums1),
        tuple(part(4, taps) for taps in TAPS[0] * 2),
        scratch=windows * 4 + staged,
        mib=16,
        ops=4,
    )
    keeps1 = res[3:6]
    gots1 = [None] * 3
    for o in (2, 0, 1):
        gots1[o] = exchange(res[o], ORDERS[o][0])
    final, mark = call(
        last_late_kernel,
        f"late_{TICKS - 1}",
        (taps, *g1s),
        (jax.ShapeDtypeStruct((2, PIX, CH), BF), MARK),
        scratch=windows * 2,
        ops=2,
    )

    parts = []
    twos = tuple(part(2, taps) for taps in TAPS[1][:2])
    both = [part(1, TAPS[0][o] + TAPS[1][o]) for o in range(3)]
    res = call(fold_two_kernel, "fold_two", (*keeps2, *gots2), twos * 2, ops=FOLD_COST)
    gots2 = [exchange(res[o], ORDERS[o][1]) for o in range(2)]
    begun = call(fold_two_last_kernel, "fold_two_last", (*res[2:4], *gots2), tuple(both[:2] * 2), ops=FOLD_COST)
    firsts = []
    order = [mark]
    for o in range(3):
        send, keep = call(fold_in, f"fold_one_{o}", (keeps1[o], gots1[o]), (part(2, TAPS[0][o]),) * 2, after=order[-1:])
        firsts.append(keep)
        order.append(keep)
        gots1[o] = exchange(send, ORDERS[o][1])
    lasts = []
    for o in range(3):
        send, keep = call(
            functools.partial(fold_one_last_kernel, o),
            f"fold_one_last_{o}",
            (firsts[o], gots1[o], *(begun[o::2] if o < 2 else ())),
            (both[o],) * 2,
            aliases={2: 0, 3: 1} if o < 2 else {},
            after=lasts[-1:],
        )
        lasts.append(keep)
        parts += [keep, exchange(send, ORDERS[o][2])]
    scale = 1.0 / math.sqrt(TICKS * DP * PIX)
    some = call(
        functools.partial(finish_some_kernel, scale),
        "finish_some",
        tuple(parts[:4]),
        jax.ShapeDtypeStruct((2, 2, 9, SHARE, CH), F32),
        ops=FOLD_COST,
    )
    grads = call(
        functools.partial(finish_kernel, scale),
        "finish",
        (some, *parts[4:]),
        jax.ShapeDtypeStruct((2, 2, 9, SHARE, CH), F32),
    )
    return (
        final.reshape(2, 1, 1, ROWS, COLS, CH),
        grads.reshape(2, 1, 2, 9, SHARE, CH),
    )


def solution(mesh):
    placed = (
        P(None, "section", "dp", None, None, None),
        P(None, "dp", None, None, None),
        P(None, "section", None, "dp", None, None, None),
        P(None, "section", None, "dp", None, None, None),
        P(None, "section", None, "dp", None, None, None),
        P(None, "section", None, None, None, None),
        P(),
    )
    return jax.shard_map(
        on_device,
        mesh=mesh,
        in_specs=placed,
        out_specs=(
            P(None, "section", "dp", None, None, None),
            P(None, "section", None, None, "dp", None),
        ),
        check_vma=False,
    )
```

```python
import functools
import math

import jax
import jax.numpy as jnp
from jax import lax
from jax.experimental import pallas as pl
from jax.experimental.pallas import tpu as pltpu
from jax.sharding import PartitionSpec as P

TICKS = 4
ROWS = 16
COLS = 32
PIX = ROWS * COLS
CH = 256
DP = 8
COST = 2 * 512 * 9 * 256 * 256
FOLD_COST = 16
PREPARE_KIB = 54016
SHARE = CH // DP
BF = jnp.bfloat16
F32 = jnp.float32
NT = (((1,), (1,)), ((), ()))

PAIRS = {
    "a": [(d, (d & 4) + ((d & 3) ^ 1)) for d in range(DP)],
    "b": [(d, (d & 4) + 3 - (d & 3)) for d in range(DP)],
    "y": [(d, d ^ 4) for d in range(DP)],
}
ORDERS = ("aby", "bya", "yab")
TAPS = ((3, 2, 4), (5, 4, 0))
FIRST = tuple(tuple(sum(taps[:o]) for o in range(3)) for taps in TAPS)

VM = pl.BlockSpec(memory_space=pltpu.VMEM)
SM = pl.BlockSpec(memory_space=pltpu.SMEM)
HB = pl.BlockSpec(memory_space=pltpu.HBM)
FIELD = jax.ShapeDtypeStruct((PIX, CH), BF)
MARK = jax.ShapeDtypeStruct((8, 128), F32)
SUMS = jax.ShapeDtypeStruct((9, CH, CH), F32)
WINDOWS = pltpu.VMEM((3, PIX + 2 * COLS, CH), BF)


def half_of(role):
    odd = lax.axis_index("section") & 1
    return odd if role == 0 else 1 - odd


def call(kernel, name, given, outs, scratch=(), mib=8, aliases={}, ops=1, after=()):
    n_given = len(given)

    def body(*refs):
        kernel(*refs[:n_given], *refs[n_given + len(after) :])

    return pl.pallas_call(
        body if after else kernel,
        out_shape=outs,
        in_specs=[VM] * n_given + [pl.BlockSpec(memory_space=pl.ANY)] * len(after),
        out_specs=jax.tree.map(lambda _: VM, outs),
        scratch_shapes=list(scratch),
        input_output_aliases=aliases,
        compiler_params=pltpu.CompilerParams(vmem_limit_bytes=mib << 20),
        cost_estimate=pl.CostEstimate(flops=ops * COST, bytes_accessed=1024, transcendentals=0),
        name=name,
    )(*given, *after)


def clear_edges(win):
    edge = jnp.zeros((3, COLS, CH), BF)
    win[:, 0:COLS, :] = edge
    win[:, COLS + PIX : 2 * COLS + PIX, :] = edge


def fill_windows(win, field):
    clear_edges(win)
    col = lax.broadcasted_iota(jnp.int32, field.shape, 0) & (COLS - 1)
    win[0, COLS : COLS + PIX, :] = jnp.where(col == 0, 0.0, pltpu.roll(field, 1, 0)).astype(BF)
    win[1, COLS : COLS + PIX, :] = field.astype(BF)
    win[2, COLS : COLS + PIX, :] = jnp.where(col == COLS - 1, 0.0, pltpu.roll(field, PIX - 1, 0)).astype(BF)


def tap_of(win, k):
    dy, dx = divmod(k, 3)
    return win[dx, dy * COLS : dy * COLS + PIX, :]


def conv(win, taps, base):
    total = None
    for k in range(9):
        term = lax.dot_general(tap_of(win, k), taps[base + 8 - k], NT, preferred_element_type=F32)
        total = term if total is None else total + term
    return total


def slot_of(table, role, tick):
    half = half_of(role)
    column = half * lax.axis_size("section") + lax.axis_index("section")
    place = lax.broadcasted_iota(jnp.int32, table.shape, 1) == column
    row = lax.broadcasted_iota(jnp.int32, table.shape, 0) == tick
    return half * 4 + jnp.sum(jnp.where(place & row, table[...], 0))


def add_up(role, tick, got, other, objective):
    total = got[...].astype(F32)
    encoder = half_of(role) == 0
    total = total + jnp.where(encoder, other[...].astype(F32), 0.0)
    if role == 1:
        first = lax.axis_index("section") == 0
        total = jnp.where(first, objective[tick - 1].astype(F32), total)
    return total


def prepare_kernel(table, *refs):
    del table
    fields, laters, earlies = refs[0:2], refs[2:4], refs[4:6]
    g2s, masks = refs[6:8], refs[8:10]
    for role in range(2):
        g2s[role][...] = jnp.where(laters[role][0] > 0, fields[role][0], jnp.zeros((), BF))
        masks[role][...] = earlies[role][0]


def prepare(table, pending, pre1, pre2):
    def at_half(role, i, table):
        return half_of(role), 0, 0

    def at_slot(role, i, table):
        half = half_of(role)
        return 4 * half + table[0, half * lax.axis_size("section") + lax.axis_index("section")], 0, 0

    def blocks(place):
        return [pl.BlockSpec((1, PIX, CH), functools.partial(place, role)) for role in range(2)]

    return pl.pallas_call(
        prepare_kernel,
        grid_spec=pltpu.PrefetchScalarGridSpec(
            num_scalar_prefetch=1,
            grid=(1,),
            in_specs=blocks(at_half) + blocks(at_slot) + blocks(at_slot),
            out_specs=[VM] * 4,
        ),
        out_shape=[FIELD] * 4,
        compiler_params=pltpu.CompilerParams(vmem_limit_bytes=PREPARE_KIB << 10),
        cost_estimate=pl.CostEstimate(flops=1, bytes_accessed=1024, transcendentals=0),
        name="prepare",
    )(table, pending, pending, pre2, pre2, pre1, pre1)


def early_of_kernel(role, mask, taps, g2, g1_out, win):
    fill_windows(win, g2[...].astype(F32))
    g1_out[...] = jnp.where(mask[...] > 0, conv(win, taps, 18 * half_of(role) + 9), 0.0).astype(BF)


def early_kernel(role, tick, table, pre1, pre2, taps, *refs):
    given = refs[:-3]
    g2_out, g1_out, win = refs[-3:]
    slot = slot_of(table, role, tick)
    g2 = add_up(role, tick, *given, *([None] * (3 - len(given))))
    g2 = jnp.where(pre2[slot] > 0, g2, 0.0)
    g2_out[...] = g2.astype(BF)
    fill_windows(win, g2)
    g1_out[...] = jnp.where(pre1[slot] > 0, conv(win, taps, 18 * half_of(role) + 9), 0.0).astype(BF)


def late_kernel(role, taps, g1, out, win):
    fill_windows(win, g1[...].astype(F32))
    out[...] = conv(win, taps, 18 * half_of(role)).astype(BF)


def tap_grads(wins, xs, fields):
    for win, field in zip(wins, fields):
        fill_windows(win, field)
    xt = jnp.concatenate([x.T for x in xs], axis=1)
    for k in range(9):
        right = jnp.concatenate([tap_of(win, 8 - k) for win in wins], axis=0)
        yield k, jnp.dot(xt, right, preferred_element_type=F32)


def left_side(which, saved, slot):
    x = saved[slot]
    return jnp.maximum(x, jnp.zeros((), BF)) if which else x


def wgrad_kernel(which, role, table, saved, *refs):
    ticks = len(refs) // 2
    fields, new, wins = refs[:ticks], refs[ticks], refs[ticks + 1 :]
    xs = [left_side(which, saved, slot_of(table, role, tick)) for tick in range(ticks)]
    for k, term in tap_grads(wins, xs, [field[...].astype(F32) for field in fields]):
        new[k] = term


def replica_at(order, r):
    me = lax.axis_index("dp")
    bit = {order[i]: (r >> (2 - i)) & 1 for i in range(3)}
    y = (me >> 2) & 1
    z = me & 3
    beta = (z >> 1) & 1
    alpha = (z & 1) ^ beta
    alpha = alpha ^ bit["a"]
    beta = beta ^ bit["b"]
    return (y ^ bit["y"]) * 4 + 2 * beta + (alpha ^ beta)


def put_shares(staged, piece, k, sends, keeps, role):
    o = sum(k >= first for first in FIRST[piece][1:])
    at = k - FIRST[piece][o]
    for r in range(DP):
        row = pl.multiple_of(replica_at(ORDERS[o], r) * SHARE, SHARE)
        share = staged[k, pl.ds(row, SHARE), :].astype(BF)
        if r >= 4:
            sends[o][r - 4, role, at] = share
        else:
            keeps[o][r, role, at] = share


def last_two_kernel(table, pre1, pre2, objective, *refs):
    given, olds = refs[:4], refs[4:6]
    sends, keeps, g2s = refs[6:8], refs[8:10], refs[10:12]
    wins, staged = refs[12:14], refs[14:16]
    tick = TICKS - 1
    for role in range(2):
        slot = slot_of(table, role, tick)
        g2 = add_up(role, tick, given[role], given[3 - role], objective)
        g2 = jnp.where(pre2[slot] > 0, g2, 0.0)
        g2s[role][...] = g2.astype(BF)
        for k, term in tap_grads(wins[role : role + 1], [left_side(1, pre1, slot)], [g2]):
            staged[role][k] = olds[role][k] + term
            put_shares(staged[role], 1, k, sends, keeps, role)


def last_early_kernel(role, table, pre1, taps, g2, g1_out, win):
    slot = slot_of(table, role, TICKS - 1)
    fill_windows(win, g2[...].astype(F32))
    g1_out[...] = jnp.where(pre1[slot] > 0, conv(win, taps, 18 * half_of(role) + 9), 0.0).astype(BF)


def last_one_kernel(table, entries, *refs):
    befores, g1s, olds = refs[:2], refs[2:4], refs[4:6]
    sends, keeps = refs[6:9], refs[9:12]
    wins, staged = refs[12:16], refs[16:18]
    for role in range(2):
        xs = [left_side(0, entries, slot_of(table, role, tick)) for tick in (TICKS - 2, TICKS - 1)]
        fields = [befores[role][...].astype(F32), g1s[role][...].astype(F32)]
        for k, term in tap_grads(wins[2 * role : 2 * role + 2], xs, fields):
            staged[role][k] = olds[role][k] + term
            put_shares(staged[role], 0, k, sends, keeps, role)


def last_late_kernel(taps, g1_zero, g1_one, out, mark, *wins):
    mark[...] = jnp.zeros(MARK.shape, F32)
    for role in range(2):
        half = half_of(role)
        fill_windows(wins[role], (g1_zero, g1_one)[role][...].astype(F32))
        out[half] = conv(wins[role], taps, 18 * half).astype(BF)


def fold_in(keep, got, send, left):
    half = keep.shape[0] // 2
    total = keep[...].astype(F32) + got[...].astype(F32)
    left[...] = total[:half].astype(BF)
    send[...] = total[half:].astype(BF)


def fold_two_kernel(*refs):
    for o in range(2):
        fold_in(*refs[o::2])


def fold_two_last_kernel(*refs):
    for o in range(2):
        keep, got, send, left = refs[o::2]
        fold_in(keep, got, send.at[:, :, TAPS[0][o] :], left.at[:, :, TAPS[0][o] :])


def fold_one_last_kernel(o, *refs):
    keep, got = refs[:2]
    send, left = refs[-2:]
    fold_in(keep, got, send.at[:, :, : TAPS[0][o]], left.at[:, :, : TAPS[0][o]])


def finish_order(scale, o, keep, got, out):
    total = keep[0].astype(F32) + got[0].astype(F32)
    for role in range(2):
        for piece in range(2):
            taps, first = TAPS[piece][o], FIRST[piece][o]
            if taps:
                low = TAPS[0][o] * piece
                out[half_of(role), piece, first : first + taps] = total[role, low : low + taps] * scale


def finish_some_kernel(scale, *refs):
    for o in range(2):
        finish_order(scale, o, *refs[2 * o : 2 * o + 2], refs[-1])


def finish_kernel(scale, some, keep, got, out):
    for piece in range(2):
        first = FIRST[piece][2]
        out[:, piece, 0:first] = some[:, piece, 0:first]
    finish_order(scale, 2, keep, got, out)


def relay(block, role):
    levels = lax.axis_size("section")
    pairs = [(i, i + 1) for i in range(1 - role, levels - 1, 2)]
    return lax.ppermute(block, "section", pairs + [(b, a) for a, b in pairs])


def exchange(block, step):
    return lax.ppermute(block, "dp", PAIRS[step])


def on_device(
    pending_adjoints,
    objective_adjoints,
    kept_block_entries,
    kept_early_presums,
    kept_later_presums,
    filter_taps,
    slot_timetable,
):
    table = slot_timetable
    entries = kept_block_entries.reshape(8, PIX, CH)
    pre1 = kept_early_presums.reshape(8, PIX, CH)
    pre2 = kept_later_presums.reshape(8, PIX, CH)
    taps = filter_taps.reshape(36, CH, CH)
    pending = pending_adjoints.reshape(2, PIX, CH)
    objective = objective_adjoints.reshape(TICKS - 1, PIX, CH)
    windows = [WINDOWS]

    all_g2s, all_g1s = [], []

    def early_sums(which, saved, fields):
        return [
            call(
                functools.partial(wgrad_kernel, which, role),
                f"wgrad{which + 1}_{role}",
                (table, saved, *[field[role] for field in fields]),
                SUMS,
                scratch=windows * len(fields),
                mib=12,
                ops=len(fields),
            )
            for role in range(2)
        ]

    gots = outs = None
    prepared = prepare(table, pending, pre1, pre2)
    for tick in range(TICKS - 1):
        g2s, g1s, new_outs, new_gots = [], [], [], []
        for role in range(2):
            if tick == 0:
                g2, mask = prepared[role], prepared[2 + role]
                g1 = call(
                    functools.partial(early_of_kernel, role),
                    f"early_{role}_0",
                    (mask, taps, g2),
                    FIELD,
                    scratch=windows,
                )
            else:
                given = (gots[1 - role], outs[1 - role]) + ((objective,) if role else ())
                g2, g1 = call(
                    functools.partial(early_kernel, role, tick),
                    f"early_{role}_{tick}",
                    (table, pre1, pre2, taps, *given),
                    (FIELD, FIELD),
                    scratch=windows,
                    after=sums1 if tick == 2 else (),
                )
            out = call(functools.partial(late_kernel, role), f"late_{role}_{tick}", (taps, g1), FIELD, scratch=windows)
            g2s.append(g2)
            g1s.append(g1)
            new_outs.append(out)
            new_gots.append(relay(out, role))
        gots, outs = new_gots, new_outs
        all_g2s.append(g2s)
        all_g1s.append(g1s)
        if tick == 1:
            sums1 = early_sums(0, entries, all_g1s)
    sums2 = early_sums(1, pre1, all_g2s)

    def part(chunks, taps):
        return jax.ShapeDtypeStruct((chunks, 2, taps, SHARE, CH), BF)

    staged = [pltpu.VMEM((9, CH, CH), F32)] * 2
    res = call(
        last_two_kernel,
        "last_two",
        (table, pre1, pre2, objective, gots[1], gots[0], *outs, *sums2),
        tuple(part(4, taps) for taps in TAPS[1][:2] * 2) + (FIELD,) * 2,
        scratch=windows * 2 + staged,
        mib=16,
        ops=2,
    )
    keeps2, g2s = res[2:4], res[4:6]
    gots2 = [exchange(res[o], ORDERS[o][0]) for o in range(2)]
    g1s = [
        call(
            functools.partial(last_early_kernel, role),
            f"early_{role}_{TICKS - 1}",
            (table, pre1, taps, g2s[role]),
            FIELD,
            scratch=windows,
        )
        for role in range(2)
    ]
    res = call(
        last_one_kernel,
        "last_one",
        (table, entries, *all_g1s[-1], *g1s, *sums1),
        tuple(part(4, taps) for taps in TAPS[0] * 2),
        scratch=windows * 4 + staged,
        mib=16,
        ops=4,
    )
    keeps1 = res[3:6]
    gots1 = [None] * 3
    for o in (2, 0, 1):
        gots1[o] = exchange(res[o], ORDERS[o][0])
    final, mark = call(
        last_late_kernel,
        f"late_{TICKS - 1}",
        (taps, *g1s),
        (jax.ShapeDtypeStruct((2, PIX, CH), BF), MARK),
        scratch=windows * 2,
        ops=2,
    )

    parts = []
    twos = tuple(part(2, taps) for taps in TAPS[1][:2])
    both = [part(1, TAPS[0][o] + TAPS[1][o]) for o in range(3)]
    res = call(fold_two_kernel, "fold_two", (*keeps2, *gots2), twos * 2, ops=FOLD_COST)
    gots2 = [exchange(res[o], ORDERS[o][1]) for o in range(2)]
    begun = call(fold_two_last_kernel, "fold_two_last", (*res[2:4], *gots2), tuple(both[:2] * 2), ops=FOLD_COST)
    firsts = []
    order = [mark]
    for o in range(3):
        send, keep = call(fold_in, f"fold_one_{o}", (keeps1[o], gots1[o]), (part(2, TAPS[0][o]),) * 2, after=order[-1:])
        firsts.append(keep)
        order.append(keep)
        gots1[o] = exchange(send, ORDERS[o][1])
    lasts = []
    for o in range(3):
        send, keep = call(
            functools.partial(fold_one_last_kernel, o),
            f"fold_one_last_{o}",
            (firsts[o], gots1[o], *(begun[o::2] if o < 2 else ())),
            (both[o],) * 2,
            aliases={2: 0, 3: 1} if o < 2 else {},
            after=lasts[-1:],
        )
        lasts.append(keep)
        parts += [keep, exchange(send, ORDERS[o][2])]
    scale = 1.0 / math.sqrt(TICKS * DP * PIX)
    some = call(
        functools.partial(finish_some_kernel, scale),
        "finish_some",
        tuple(parts[:4]),
        jax.ShapeDtypeStruct((2, 2, 9, SHARE, CH), F32),
        ops=FOLD_COST,
    )
    grads = call(
        functools.partial(finish_kernel, scale),
        "finish",
        (some, *parts[4:]),
        jax.ShapeDtypeStruct((2, 2, 9, SHARE, CH), F32),
    )
    return (
        final.reshape(2, 1, 1, ROWS, COLS, CH),
        grads.reshape(2, 1, 2, 9, SHARE, CH),
    )


def solution(mesh):
    placed = (
        P(None, "section", "dp", None, None, None),
        P(None, "dp", None, None, None),
        P(None, "section", None, "dp", None, None, None),
        P(None, "section", None, "dp", None, None, None),
        P(None, "section", None, "dp", None, None, None),
        P(None, "section", None, None, None, None),
        P(),
    )
    return jax.shard_map(
        on_device,
        mesh=mesh,
        in_specs=placed,
        out_specs=(
            P(None, "section", "dp", None, None, None),
            P(None, "section", None, None, "dp", None),
        ),
        check_vma=False,
    )
```

```python
import functools
import math

import jax
import jax.numpy as jnp
from jax import lax
from jax.experimental import pallas as pl
from jax.experimental.pallas import tpu as pltpu
from jax.sharding import PartitionSpec as P

TICKS = 4
ROWS = 16
COLS = 32
PIX = ROWS * COLS
CH = 256
DP = 8
COST = 2 * 512 * 9 * 256 * 256
FOLD_COST = 16
PREPARE_KIB = 54016
SHARE = CH // DP
BF = jnp.bfloat16
F32 = jnp.float32
NT = (((1,), (1,)), ((), ()))

PAIRS = {
    "a": [(d, (d & 4) + ((d & 3) ^ 1)) for d in range(DP)],
    "b": [(d, (d & 4) + 3 - (d & 3)) for d in range(DP)],
    "y": [(d, d ^ 4) for d in range(DP)],
}
ORDERS = ("ayb", "bay", "yba")

VM = pl.BlockSpec(memory_space=pltpu.VMEM)
SM = pl.BlockSpec(memory_space=pltpu.SMEM)
HB = pl.BlockSpec(memory_space=pltpu.HBM)
FIELD = jax.ShapeDtypeStruct((PIX, CH), BF)
MARK = jax.ShapeDtypeStruct((8, 128), F32)
SUMS = jax.ShapeDtypeStruct((9, CH, CH), F32)
WINDOWS = pltpu.VMEM((3, PIX + 2 * COLS, CH), BF)


def half_of(role):
    odd = lax.axis_index("section") & 1
    return odd if role == 0 else 1 - odd


def call(kernel, name, given, outs, scratch=(), mib=8, aliases={}, ops=1, after=()):
    n_given = len(given)

    def body(*refs):
        kernel(*refs[:n_given], *refs[n_given + len(after) :])

    return pl.pallas_call(
        body if after else kernel,
        out_shape=outs,
        in_specs=[VM] * n_given + [pl.BlockSpec(memory_space=pl.ANY)] * len(after),
        out_specs=jax.tree.map(lambda _: VM, outs),
        scratch_shapes=list(scratch),
        input_output_aliases=aliases,
        compiler_params=pltpu.CompilerParams(vmem_limit_bytes=mib << 20),
        cost_estimate=pl.CostEstimate(flops=ops * COST, bytes_accessed=1024, transcendentals=0),
        name=name,
    )(*given, *after)


def clear_edges(win):
    edge = jnp.zeros((3, COLS, CH), BF)
    win[:, 0:COLS, :] = edge
    win[:, COLS + PIX : 2 * COLS + PIX, :] = edge


def fill_windows(win, field):
    clear_edges(win)
    col = lax.broadcasted_iota(jnp.int32, field.shape, 0) & (COLS - 1)
    win[0, COLS : COLS + PIX, :] = jnp.where(col == 0, 0.0, pltpu.roll(field, 1, 0)).astype(BF)
    win[1, COLS : COLS + PIX, :] = field.astype(BF)
    win[2, COLS : COLS + PIX, :] = jnp.where(col == COLS - 1, 0.0, pltpu.roll(field, PIX - 1, 0)).astype(BF)


def tap_of(win, k):
    dy, dx = divmod(k, 3)
    return win[dx, dy * COLS : dy * COLS + PIX, :]


def conv(win, taps, base):
    total = None
    for k in range(9):
        term = lax.dot_general(tap_of(win, k), taps[base + 8 - k], NT, preferred_element_type=F32)
        total = term if total is None else total + term
    return total


def slot_of(table, role, tick):
    half = half_of(role)
    column = half * lax.axis_size("section") + lax.axis_index("section")
    place = lax.broadcasted_iota(jnp.int32, table.shape, 1) == column
    row = lax.broadcasted_iota(jnp.int32, table.shape, 0) == tick
    return half * 4 + jnp.sum(jnp.where(place & row, table[...], 0))


def add_up(role, tick, got, other, objective):
    total = got[...].astype(F32)
    encoder = half_of(role) == 0
    total = total + jnp.where(encoder, other[...].astype(F32), 0.0)
    if role == 1:
        first = lax.axis_index("section") == 0
        total = jnp.where(first, objective[tick - 1].astype(F32), total)
    return total


def prepare_kernel(table, *refs):
    del table
    fields, laters, earlies = refs[0:2], refs[2:4], refs[4:6]
    g2s, masks = refs[6:8], refs[8:10]
    for role in range(2):
        g2s[role][...] = jnp.where(laters[role][0] > 0, fields[role][0], jnp.zeros((), BF))
        masks[role][...] = earlies[role][0]


def prepare(table, pending, pre1, pre2):
    def at_half(role, i, table):
        return half_of(role), 0, 0

    def at_slot(role, i, table):
        half = half_of(role)
        return 4 * half + table[0, half * lax.axis_size("section") + lax.axis_index("section")], 0, 0

    def blocks(place):
        return [pl.BlockSpec((1, PIX, CH), functools.partial(place, role)) for role in range(2)]

    return pl.pallas_call(
        prepare_kernel,
        grid_spec=pltpu.PrefetchScalarGridSpec(
            num_scalar_prefetch=1,
            grid=(1,),
            in_specs=blocks(at_half) + blocks(at_slot) + blocks(at_slot),
            out_specs=[VM] * 4,
        ),
        out_shape=[FIELD] * 4,
        compiler_params=pltpu.CompilerParams(vmem_limit_bytes=PREPARE_KIB << 10),
        cost_estimate=pl.CostEstimate(flops=1, bytes_accessed=1024, transcendentals=0),
        name="prepare",
    )(table, pending, pending, pre2, pre2, pre1, pre1)


def early_of_kernel(role, mask, taps, g2, g1_out, win):
    fill_windows(win, g2[...].astype(F32))
    g1_out[...] = jnp.where(mask[...] > 0, conv(win, taps, 18 * half_of(role) + 9), 0.0).astype(BF)


def early_kernel(role, tick, table, pre1, pre2, taps, *refs):
    given = refs[:-3]
    g2_out, g1_out, win = refs[-3:]
    slot = slot_of(table, role, tick)
    g2 = add_up(role, tick, *given, *([None] * (3 - len(given))))
    g2 = jnp.where(pre2[slot] > 0, g2, 0.0)
    g2_out[...] = g2.astype(BF)
    fill_windows(win, g2)
    g1_out[...] = jnp.where(pre1[slot] > 0, conv(win, taps, 18 * half_of(role) + 9), 0.0).astype(BF)


def late_kernel(role, taps, g1, out, win):
    fill_windows(win, g1[...].astype(F32))
    out[...] = conv(win, taps, 18 * half_of(role)).astype(BF)


def tap_grads(wins, xs, fields):
    for win, field in zip(wins, fields):
        fill_windows(win, field)
    xt = jnp.concatenate([x.T for x in xs], axis=1)
    for k in range(9):
        right = jnp.concatenate([tap_of(win, 8 - k) for win in wins], axis=0)
        yield k, jnp.dot(xt, right, preferred_element_type=F32)


def left_side(which, saved, slot):
    x = saved[slot]
    return jnp.maximum(x, jnp.zeros((), BF)) if which else x


def wgrad_kernel(which, role, table, saved, *refs):
    ticks = len(refs) // 2
    fields, new, wins = refs[:ticks], refs[ticks], refs[ticks + 1 :]
    xs = [left_side(which, saved, slot_of(table, role, tick)) for tick in range(ticks)]
    for k, term in tap_grads(wins, xs, [field[...].astype(F32) for field in fields]):
        new[k] = term


def replica_at(order, r):
    me = lax.axis_index("dp")
    bit = {order[i]: (r >> (2 - i)) & 1 for i in range(3)}
    y = (me >> 2) & 1
    z = me & 3
    beta = (z >> 1) & 1
    alpha = (z & 1) ^ beta
    alpha = alpha ^ bit["a"]
    beta = beta ^ bit["b"]
    return (y ^ bit["y"]) * 4 + 2 * beta + (alpha ^ beta)


def put_shares(staged, k, sends, keeps, role):
    o, at = divmod(k, 3)
    for r in range(DP):
        row = pl.multiple_of(replica_at(ORDERS[o], r) * SHARE, SHARE)
        share = staged[k, pl.ds(row, SHARE), :].astype(BF)
        if r >= 4:
            sends[o][r - 4, role, at] = share
        else:
            keeps[o][r, role, at] = share


def last_two_kernel(table, pre1, pre2, objective, *refs):
    given, olds = refs[:4], refs[4:6]
    sends, keeps, g2s = refs[6:9], refs[9:12], refs[12:14]
    wins, staged = refs[14:16], refs[16:18]
    tick = TICKS - 1
    for role in range(2):
        slot = slot_of(table, role, tick)
        g2 = add_up(role, tick, given[role], given[3 - role], objective)
        g2 = jnp.where(pre2[slot] > 0, g2, 0.0)
        g2s[role][...] = g2.astype(BF)
        for k, term in tap_grads(wins[role : role + 1], [left_side(1, pre1, slot)], [g2]):
            staged[role][k] = olds[role][k] + term
            put_shares(staged[role], k, sends, keeps, role)


def last_early_kernel(role, table, pre1, taps, g2, g1_out, win):
    slot = slot_of(table, role, TICKS - 1)
    fill_windows(win, g2[...].astype(F32))
    g1_out[...] = jnp.where(pre1[slot] > 0, conv(win, taps, 18 * half_of(role) + 9), 0.0).astype(BF)


def last_one_kernel(table, entries, *refs):
    befores, g1s, olds = refs[:2], refs[2:4], refs[4:6]
    sends, keeps = refs[6:9], refs[9:12]
    wins, staged = refs[12:16], refs[16:18]
    for role in range(2):
        xs = [left_side(0, entries, slot_of(table, role, tick)) for tick in (TICKS - 2, TICKS - 1)]
        fields = [befores[role][...].astype(F32), g1s[role][...].astype(F32)]
        for k, term in tap_grads(wins[2 * role : 2 * role + 2], xs, fields):
            staged[role][k] = olds[role][k] + term
            put_shares(staged[role], k, sends, keeps, role)


def last_late_kernel(taps, g1_zero, g1_one, out, mark, *wins):
    mark[...] = jnp.zeros(MARK.shape, F32)
    for role in range(2):
        half = half_of(role)
        fill_windows(wins[role], (g1_zero, g1_one)[role][...].astype(F32))
        out[half] = conv(wins[role], taps, 18 * half).astype(BF)


def fold_in(keep, got, send, left):
    half = keep.shape[0] // 2
    total = keep[...].astype(F32) + got[...].astype(F32)
    left[...] = total[:half].astype(BF)
    send[...] = total[half:].astype(BF)


def fold_kernel(*refs):
    for o in range(3):
        fold_in(*refs[o::3])


def fold_two_last_kernel(*refs):
    for o in range(3):
        keep, got, send, left = refs[o::3]
        fold_in(keep, got, send.at[:, 1], left.at[:, 1])


def fold_one_last_kernel(keep, got, old_send, old_left, send, left):
    del old_send, old_left
    fold_in(keep, got, send.at[:, 0], left.at[:, 0])


def finish_some_kernel(scale, *refs):
    out = refs[-1]
    for o in range(2):
        keep, got = refs[2 * o : 2 * o + 2]
        total = keep[0].astype(F32) + got[0].astype(F32)
        for role in range(2):
            for piece in range(2):
                out[half_of(role), piece, 3 * o : 3 * o + 3] = total[piece, role] * scale


def finish_kernel(scale, some, keep, got, out):
    out[:, :, 0:6] = some[...]
    total = keep[0].astype(F32) + got[0].astype(F32)
    for role in range(2):
        for piece in range(2):
            out[half_of(role), piece, 6:9] = total[piece, role] * scale


def relay(block, role):
    levels = lax.axis_size("section")
    pairs = [(i, i + 1) for i in range(1 - role, levels - 1, 2)]
    return lax.ppermute(block, "section", pairs + [(b, a) for a, b in pairs])


def exchange(block, step):
    return lax.ppermute(block, "dp", PAIRS[step])


def on_device(
    pending_adjoints,
    objective_adjoints,
    kept_block_entries,
    kept_early_presums,
    kept_later_presums,
    filter_taps,
    slot_timetable,
):
    table = slot_timetable
    entries = kept_block_entries.reshape(8, PIX, CH)
    pre1 = kept_early_presums.reshape(8, PIX, CH)
    pre2 = kept_later_presums.reshape(8, PIX, CH)
    taps = filter_taps.reshape(36, CH, CH)
    pending = pending_adjoints.reshape(2, PIX, CH)
    objective = objective_adjoints.reshape(TICKS - 1, PIX, CH)
    windows = [WINDOWS]

    all_g2s, all_g1s = [], []

    def early_sums(which, saved, fields):
        return [
            call(
                functools.partial(wgrad_kernel, which, role),
                f"wgrad{which + 1}_{role}",
                (table, saved, *[field[role] for field in fields]),
                SUMS,
                scratch=windows * len(fields),
                mib=12,
                ops=len(fields),
            )
            for role in range(2)
        ]

    gots = outs = None
    prepared = prepare(table, pending, pre1, pre2)
    for tick in range(TICKS - 1):
        g2s, g1s, new_outs, new_gots = [], [], [], []
        for role in range(2):
            if tick == 0:
                g2, mask = prepared[role], prepared[2 + role]
                g1 = call(
                    functools.partial(early_of_kernel, role),
                    f"early_{role}_0",
                    (mask, taps, g2),
                    FIELD,
                    scratch=windows,
                )
            else:
                given = (gots[1 - role], outs[1 - role]) + ((objective,) if role else ())
                g2, g1 = call(
                    functools.partial(early_kernel, role, tick),
                    f"early_{role}_{tick}",
                    (table, pre1, pre2, taps, *given),
                    (FIELD, FIELD),
                    scratch=windows,
                    after=sums1 if tick == 2 else (),
                )
            out = call(functools.partial(late_kernel, role), f"late_{role}_{tick}", (taps, g1), FIELD, scratch=windows)
            g2s.append(g2)
            g1s.append(g1)
            new_outs.append(out)
            new_gots.append(relay(out, role))
        gots, outs = new_gots, new_outs
        all_g2s.append(g2s)
        all_g1s.append(g1s)
        if tick == 1:
            sums1 = early_sums(0, entries, all_g1s)
    sums2 = early_sums(1, pre1, all_g2s)

    part = jax.ShapeDtypeStruct((4, 2, 3, SHARE, CH), BF)
    staged = [pltpu.VMEM((9, CH, CH), F32)] * 2
    res = call(
        last_two_kernel,
        "last_two",
        (table, pre1, pre2, objective, gots[1], gots[0], *outs, *sums2),
        (part,) * 6 + (FIELD,) * 2,
        scratch=windows * 2 + staged,
        mib=16,
        ops=2,
    )
    keeps2, g2s = res[3:6], res[6:8]
    gots2 = [exchange(res[o], ORDERS[o][0]) for o in range(3)]
    g1s = [
        call(
            functools.partial(last_early_kernel, role),
            f"early_{role}_{TICKS - 1}",
            (table, pre1, taps, g2s[role]),
            FIELD,
            scratch=windows,
        )
        for role in range(2)
    ]
    res = call(
        last_one_kernel,
        "last_one",
        (table, entries, *all_g1s[-1], *g1s, *sums1),
        (part,) * 6,
        scratch=windows * 4 + staged,
        mib=16,
        ops=4,
    )
    keeps1 = res[3:6]
    gots1 = [exchange(res[o], ORDERS[o][0]) for o in range(3)]
    final, mark = call(
        last_late_kernel,
        f"late_{TICKS - 1}",
        (taps, *g1s),
        (jax.ShapeDtypeStruct((2, PIX, CH), BF), MARK),
        scratch=windows * 2,
        ops=2,
    )

    parts = []
    part2 = jax.ShapeDtypeStruct((2, 2, 3, SHARE, CH), BF)
    part3 = jax.ShapeDtypeStruct((1, 2, 2, 3, SHARE, CH), BF)
    res = call(fold_kernel, "fold_two", (*keeps2, *gots2), (part2,) * 6, ops=FOLD_COST)
    gots2 = [exchange(res[o], ORDERS[o][1]) for o in range(3)]
    begun = call(fold_two_last_kernel, "fold_two_last", (*res[3:6], *gots2), (part3,) * 6, ops=FOLD_COST)
    firsts = []
    order = [mark]
    for o in range(3):
        send, keep = call(fold_in, f"fold_one_{o}", (keeps1[o], gots1[o]), (part2, part2), after=order[-1:])
        firsts.append(keep)
        order.append(keep)
        gots1[o] = exchange(send, ORDERS[o][1])
    lasts = []
    for o in range(3):
        send, keep = call(
            fold_one_last_kernel,
            f"fold_one_last_{o}",
            (firsts[o], gots1[o], begun[o], begun[3 + o]),
            (part3, part3),
            aliases={2: 0, 3: 1},
            after=lasts[-1:],
        )
        lasts.append(keep)
        parts += [keep, exchange(send, ORDERS[o][2])]
    scale = 1.0 / math.sqrt(TICKS * DP * PIX)
    some = call(
        functools.partial(finish_some_kernel, scale),
        "finish_some",
        tuple(parts[:4]),
        jax.ShapeDtypeStruct((2, 2, 6, SHARE, CH), F32),
        ops=FOLD_COST,
    )
    grads = call(
        functools.partial(finish_kernel, scale),
        "finish",
        (some, *parts[4:]),
        jax.ShapeDtypeStruct((2, 2, 9, SHARE, CH), F32),
    )
    return (
        final.reshape(2, 1, 1, ROWS, COLS, CH),
        grads.reshape(2, 1, 2, 9, SHARE, CH),
    )


def solution(mesh):
    placed = (
        P(None, "section", "dp", None, None, None),
        P(None, "dp", None, None, None),
        P(None, "section", None, "dp", None, None, None),
        P(None, "section", None, "dp", None, None, None),
        P(None, "section", None, "dp", None, None, None),
        P(None, "section", None, None, None, None),
        P(),
    )
    return jax.shard_map(
        on_device,
        mesh=mesh,
        in_specs=placed,
        out_specs=(
            P(None, "section", "dp", None, None, None),
            P(None, "section", None, None, "dp", None),
        ),
        check_vma=False,
    )
```
